128 devices in a mesh: sec: 32 (over z, x, core), col: 4 (over y).
Axes of the slice: x: 4, y: 4, z: 4, core: 2. Of those that a mesh axis runs over, the one named last changes fastest.
Arguments:
- right_sides: float32 [32, 4, 20, 128, 256], P('sec', 'col'), may hold values from -6 to 6
- diag_inverse: float32 [32, 4, 20, 128, 128], P('sec', 'col'), may hold values from -1 to 1
- coupling: float32 [32, 4, 20, 128, 128], P('sec', 'col'), may hold values from -1 to 1
- off_blocks: float32 [32, 4, 15, 16, 128, 128], P('sec', 'col'), may hold values from -0.125 to 0.125
- pattern: int32 [32, 4, 15, 16], P('sec', 'col'), may hold values from 0 to 59, as said below
Outputs:
- solution: float32 [32, 4, 20, 128, 256], P('sec', 'col')
The draws below stay inside these ranges and needn't reach their ends.
Inputs may be any that keep to these rules, and one draw needn't show every extreme that they name: `pattern`: in a device's list, entry (l - 1) * 5 + k holds 16 different positions below l * 4 * 5, that is of levels under l.
All inputs are finite; a program needn't handle non-finite values.
Results may differ from the reference program's by a relative error of at most 0.0003.
Values sent between devices are 32-bit elements; how exact they have to be, the bound alone decides.
A program may use at most 128 MiB of HBM per device.

```python
import math
import jax
import jax.numpy as jnp
from jax import lax

BS = 128
RHS = 256
LEV = 4
RL = 5
KB = 16
NB_DEV = 20
N_SEC = 32
N_COL = 4


def draw_diag_inverse(key, part):
    key = jax.random.fold_in(key, 2)
    eye = jnp.eye(BS, dtype=jnp.float32)
    shape_all = (N_SEC, N_COL, NB_DEV, BS, BS)
    spread = 0.3 / math.sqrt(BS)
    noise = jax.random.normal(key, shape_all, jnp.float32) * spread
    return 0.6 * eye + noise


def draw_coupling(key, part):
    key = jax.random.fold_in(key, 7)
    shape_all = (N_SEC, N_COL, NB_DEV, BS, BS)
    spread = 1.1 / math.sqrt(BS)
    return jax.random.truncated_normal(key, -3.5, 3.5, shape_all, jnp.float32) * spread


def draw_pattern(key, part):
    key = jax.random.fold_in(key, 5)
    row_total = (LEV - 1) * RL
    position_total = N_COL * NB_DEV
    random_keys = jax.random.randint(key, (N_SEC, N_COL, row_total, position_total), 0, 1 << 20)
    position_ids = jnp.arange(position_total, dtype=jnp.int32)
    level_of_row = jnp.arange(row_total, dtype=jnp.int32) // RL + 1
    bound_row = level_of_row * (N_COL * RL)
    scores = jnp.where(position_ids[None, :] < bound_row[:, None], random_keys * position_total + position_ids, -1)
    return lax.top_k(scores, KB)[1].astype(jnp.int32)


def level_of(key, shape, cuts, smallest, top_value):
    factor_of = 1.0
    for position, parts in cuts:
        steps = jax.random.uniform(jax.random.fold_in(jax.random.fold_in(key, 6), position), (parts,), jnp.float32, smallest / len(cuts), top_value / len(cuts))
        factor_of = factor_of * jnp.repeat(jnp.exp(steps), shape[position] // parts).reshape((-1,) + (1,) * (len(shape) - 1 - position))
    return factor_of


def centred(own_key, dims, deviation, most, split=(), kind=jnp.bfloat16):
    array = deviation * jax.random.normal(own_key, dims, jnp.float32)
    if split:
        array = array * level_of(own_key, dims, split, -0.22, 0.18)
    return jnp.clip(array, -most, most).astype(kind)


def setup_inputs(seed: int = 0) -> dict:
    splits = jax.random.split(jax.random.key(seed), 6)
    right_sides = centred(splits[0], (N_SEC, N_COL, NB_DEV, BS, RHS), 1.0, 6.0, ((0, 32), (1, 4)), jnp.float32)
    diag_inverse = draw_diag_inverse(jax.random.fold_in(splits[5], 71), 0)
    coupling = draw_coupling(jax.random.fold_in(splits[5], 71), 0)
    off_blocks = centred(splits[3], (N_SEC, N_COL, (LEV - 1) * RL, KB, BS, BS), (KB * BS) ** -0.5, 0.125, ((0, 32), (1, 4)), jnp.float32)
    pattern = draw_pattern(jax.random.fold_in(splits[5], 71), 0)
    return {"right_sides": right_sides, "diag_inverse": diag_inverse, "coupling": coupling, "off_blocks": off_blocks, "pattern": pattern}


HIGH = lax.Precision.HIGHEST


def reference(right_sides, diag_inverse, coupling, off_blocks, pattern):
    def section(previous, pieces):
        rhs_part, diag_part, couple_part, block_part, index_part = pieces
        current_all = rhs_part - jnp.einsum("cnab,bw->cnaw", couple_part, previous, precision=HIGH)
        section_table = jnp.zeros((N_COL * NB_DEV, BS, RHS), jnp.float32)
        levels_out = []
        for level_index in range(LEV):
            first_row = level_index * RL
            current = current_all[:, first_row:first_row + RL]
            if level_index > 0:
                lower_row = (level_index - 1) * RL
                picked = jnp.take(section_table, index_part[:, lower_row:lower_row + RL], axis=0)
                current = current - jnp.einsum("cpkab,cpkbw->cpaw", block_part[:, lower_row:lower_row + RL], picked, precision=HIGH)
            solved = jnp.einsum("cpab,cpbw->cpaw", diag_part[:, first_row:first_row + RL], current, precision=HIGH)
            levels_out.append(solved)
            start_row = level_index * N_COL * RL
            section_table = section_table.at[start_row:start_row + N_COL * RL].set(solved.reshape(N_COL * RL, BS, RHS))
        return section_table[-1], jnp.concatenate(levels_out, axis=1)

    initial = jnp.zeros((BS, RHS), jnp.float32)
    last_block, solution = lax.scan(section, initial, (right_sides, diag_inverse, coupling, off_blocks, pattern))
    return solution
```

```python
import functools

import jax
import jax.numpy as jnp
from jax import lax
from jax.experimental import pallas as pl
from jax.experimental.pallas import tpu as pltpu
from jax.sharding import PartitionSpec as P

LEV = 4
CHUNKS = 3
MESH = pl.DeviceIdType.MESH
F32 = jnp.float32
BF16 = jnp.bfloat16


def split(value):
    high = value.astype(BF16)
    return high, (value - high.astype(F32)).astype(BF16)


def dot(left, right):
    return jnp.dot(left, right, preferred_element_type=F32)


def dot3(left, right):
    left_high, left_low = split(left)
    right_high, right_low = split(right)
    both = dot(left_high, jnp.concatenate([right_high, right_low], axis=1))
    width = right.shape[1]
    return both[:, :width] + both[:, width:] + dot(left_low, right_high)


def section_kernel(
    pattern, right_sides, diag, coupling, off,
    y_out, w_out,
    rhs_v, diag_v, coup_v, off_v, got, table, top, in_sem, out_sem, send_sem, recv_sem,
):
    me = lax.axis_index("col")
    right, left, across = lax.rem(me + 1, 4), lax.rem(me + 3, 4), lax.rem(me + 2, 4)
    per_level = diag_v.shape[0] // LEV
    bs = diag_v.shape[1]
    half = per_level * bs // 2
    items = (LEV - 1) * CHUNKS

    def level_rows(level):
        return pl.ds(level * per_level, per_level)

    loads = []
    for level in range(LEV):
        rows = level_rows(level)
        parts = [(coupling.at[rows], coup_v.at[rows]), (diag.at[rows], diag_v.at[rows]), (right_sides.at[rows], rhs_v.at[rows])]
        if level:
            lower = level_rows(level - 1)
            parts.append((off.at[lower], off_v.at[lower]))
        loads.append([pltpu.make_async_copy(a, b, in_sem.at[level, i]) for i, (a, b) in enumerate(parts)])
    for group in loads:
        for copy in group:
            copy.start()

    barrier = pltpu.get_barrier_semaphore()
    for neighbour in (left, right):
        pl.semaphore_signal(barrier, inc=1, device_id={"col": neighbour}, device_id_type=MESH)

    lo, hi = pl.ds(0, half), pl.ds(half, half)

    def remote(item, slot, rows, index, target):
        ref = got.at[item, slot, rows]
        return pltpu.make_async_remote_copy(
            src_ref=ref, dst_ref=ref, send_sem=send_sem.at[item, index], recv_sem=recv_sem.at[item, index],
            device_id={"col": target}, device_id_type=MESH,
        )

    def own_sends(item):
        return [remote(item, me, lo, 0, right), remote(item, me, hi, 1, left), remote(item, me, hi, 2, right), remote(item, me, lo, 3, left)]

    def forwards(item):
        return [remote(item, left, lo, 4, right), remote(item, right, hi, 5, left)]

    def arrival(item, index):
        slot = (left, right, left, right, across, across)[index]
        return remote(item, slot, (lo, hi, hi, lo, lo, hi)[index], index, right)

    def forward(item):
        arrival(item, 0).wait_recv()
        go = forwards(item)
        go[0].start()
        arrival(item, 1).wait_recv()
        go[1].start()

    def finish(item):
        for index in range(2, 6):
            arrival(item, index).wait_recv()

    def to_table(level, chunk):
        item = level * CHUNKS + chunk
        base = chunk * (LEV - 1) * 4 * per_level + level * 4 * per_level

        def body(k, carry):
            for source in range(4):
                high, low = split(got[item, source, pl.ds(pl.multiple_of(k * bs, bs), bs), :])
                table[base + source * per_level + k, :, :bs] = high
                table[base + source * per_level + k, :, bs:] = low
            return carry

        lax.fori_loop(0, per_level, body, 0)

    def compute(level, chunk):
        def body(k, carry):
            row = level * per_level + k
            if chunk == 0:
                current = -coup_v[row]
            else:
                current = rhs_v[row, :, (chunk - 1) * bs : chunk * bs]
            if level:
                low_row = (level - 1) * per_level + k
                wide = jnp.zeros((bs, 2 * bs), F32)
                narrow = jnp.zeros((bs, bs), F32)
                base = chunk * (LEV - 1) * 4 * per_level
                for first in range(0, 16, 4):
                    pieces = [split(off_v[low_row, j]) for j in range(first, first + 4)]
                    picked = jnp.concatenate([table[base + pattern[low_row, j]] for j in range(first, first + 4)], axis=0)
                    wide += dot(jnp.concatenate([p[0] for p in pieces], axis=1), picked)
                    narrow += dot(jnp.concatenate([p[1] for p in pieces], axis=1), picked[:, :bs])
                current = current - (wide[:, :bs] + wide[:, bs:] + narrow)
            solved = dot3(diag_v[row], current)
            if level < LEV - 1:
                got[level * CHUNKS + chunk, me, pl.ds(pl.multiple_of(k * bs, bs), bs), :] = solved
            else:
                top[chunk, pl.ds(pl.multiple_of(k * bs, bs), bs), :] = solved
            return carry

        lax.fori_loop(0, per_level, body, 0)

    def writes(level, chunk):
        source = got.at[level * CHUNKS + chunk, me] if level < LEV - 1 else top.at[chunk]
        copies = []
        for k in range(per_level):
            row = level * per_level + k
            target = w_out.at[row] if chunk == 0 else y_out.at[row, :, pl.ds((chunk - 1) * bs, bs)]
            copies.append(pltpu.make_async_copy(source.at[pl.ds(k * bs, bs)], target, out_sem.at[level * CHUNKS + chunk, k]))
        return copies

    for copy in loads[0]:
        copy.wait()
    compute(0, 0)
    pl.semaphore_wait(barrier, 2)
    for item in range(items):
        for copy in own_sends(item):
            copy.start()
        for copy in writes(item // CHUNKS, item % CHUNKS):
            copy.start()
        following = item + 1
        if following < items:
            level, chunk = following // CHUNKS, following % CHUNKS
            if level:
                if chunk == 0:
                    for copy in loads[level]:
                        copy.wait()
                finish(following - CHUNKS)
                to_table(level - 1, chunk)
            compute(level, chunk)
        forward(item)
    for copy in loads[LEV - 1]:
        copy.wait()
    for chunk in range(CHUNKS):
        finish(items - CHUNKS + chunk)
        to_table(LEV - 2, chunk)
        compute(LEV - 1, chunk)
        for copy in writes(LEV - 1, chunk):
            copy.start()
    for item in range(items):
        for copy in own_sends(item) + forwards(item):
            copy.wait_send()
    for item in range(LEV * CHUNKS):
        for copy in writes(item // CHUNKS, item % CHUNKS):
            copy.wait()


def section_solve(right_sides, diag_inverse, coupling, off_blocks, pattern):
    rows, bs, width = right_sides.shape
    per_level = rows // LEV
    items = (LEV - 1) * CHUNKS
    any_space = pl.BlockSpec(memory_space=pl.ANY)
    return pl.pallas_call(
        section_kernel,
        out_shape=(jax.ShapeDtypeStruct((rows, bs, width), F32), jax.ShapeDtypeStruct((rows, bs, bs), F32)),
        in_specs=[pl.BlockSpec(memory_space=pltpu.SMEM)] + [any_space] * 4,
        out_specs=(any_space, any_space),
        scratch_shapes=[
            pltpu.VMEM((rows, bs, width), F32),
            pltpu.VMEM((rows, bs, bs), F32),
            pltpu.VMEM((rows, bs, bs), F32),
            pltpu.VMEM(off_blocks.shape, F32),
            pltpu.VMEM((items, 4, per_level * bs, bs), F32),
            pltpu.VMEM((CHUNKS * (LEV - 1) * 4 * per_level, bs, 2 * bs), BF16),
            pltpu.VMEM((CHUNKS, per_level * bs, bs), F32),
            pltpu.SemaphoreType.DMA((LEV, 4)),
            pltpu.SemaphoreType.DMA((LEV * CHUNKS, per_level)),
            pltpu.SemaphoreType.DMA((items, 6)),
            pltpu.SemaphoreType.DMA((items, 6)),
        ],
        compiler_params=pltpu.CompilerParams(collective_id=0, has_side_effects=True, vmem_limit_bytes=56 << 20),
        name="section_solve",
    )(pattern, right_sides, diag_inverse, coupling, off_blocks)


def scan_kernel(y_all, w_all, last_out, y_row, w_row, first, state, pair, xs, zs, in_sem, send_sem, recv_sem):
    sec, col = lax.axis_index("sec"), lax.axis_index("col")
    core = lax.rem(sec, 2)
    x = lax.rem(sec // 2, 4)
    z = sec // 8
    bs = w_row.shape[0]
    quarter = y_row.shape[1] // 4
    own_rows, map_rows = pl.ds(0, quarter), pl.ds(quarter, bs)

    def at(axis, step):
        if axis == "y":
            return {"col": lax.rem(col + step, 4)}
        if axis == "core":
            return {"sec": sec + 1 - 2 * core}
        if axis == "x":
            return {"sec": (z * 4 + lax.rem(x + step, 4)) * 2 + core}
        return {"sec": (lax.rem(z + step, 4) * 4 + x) * 2 + core}

    partners = [(axis, step) for axis in ("y", "x", "z") for step in (1, 2, 3)] + [("core", 1)]
    barrier = pltpu.get_barrier_semaphore()
    for axis, step in partners:
        pl.semaphore_signal(barrier, inc=1, device_id=at(axis, step), device_id_type=MESH)
    last_row = y_all.shape[0] - 1
    fetch = [pltpu.make_async_copy(y_all.at[last_row], y_row, in_sem.at[0]), pltpu.make_async_copy(w_all.at[last_row], w_row, in_sem.at[1])]
    for copy in fetch:
        copy.start()
    for copy in fetch:
        copy.wait()
    pl.semaphore_wait(barrier, len(partners))

    def remote(source, target, phase, axis, step):
        return pltpu.make_async_remote_copy(
            src_ref=source, dst_ref=target, send_sem=send_sem.at[phase, step], recv_sem=recv_sem.at[phase, step],
            device_id=at(axis, step), device_id_type=MESH,
        )

    shares = [remote(first.at[lax.rem(col + step, 4)], state, 0, "y", step) for step in (1, 2, 3)]

    @pl.when(col == 3)
    def _():
        map_t = w_row[...].T
        base_t = y_row[...].T
        for part in range(4):
            first[part, :quarter] = base_t[part * quarter : (part + 1) * quarter]
            first[part, quarter:] = map_t
        for copy in shares:
            copy.start()
        state[...] = first[3]
        for copy in shares:
            copy.wait_send()

    for part in range(3):

        @pl.when(col == part)
        def _(part=part):
            shares[part].wait_recv()

    def then(earlier, later):
        product = dot3(earlier, later[quarter:])
        return jnp.concatenate([product[:quarter] + later[:quarter], product[quarter:]], axis=0)

    swap = remote(state, pair, 1, "core", 1)
    swap.start()
    swap.wait()
    mine, other = state[...], pair[...]
    even = jnp.where(core == 0, mine, other)
    odd = jnp.where(core == 0, other, mine)
    both = then(even, odd)

    def spread(buffer, place, phase, axis, value):
        buffer[place] = value
        copies = [remote(buffer.at[place], buffer.at[place], phase, axis, step) for step in (1, 2, 3)]
        for copy in copies:
            copy.start()
        for step in (1, 2, 3):
            source = buffer.at[lax.rem(place + 4 - step, 4)]
            remote(source, source, phase, axis, step).wait_recv()
        return copies

    started = spread(xs, x, 2, "x", both)
    total = xs[0]
    before = jnp.where(x == 1, total, jnp.zeros_like(total))
    for place in (1, 2, 3):
        total = then(total, xs[place])
        if place < 3:
            before = jnp.where(x == place + 1, total, before)
    started += spread(zs, z, 3, "z", total)
    carried = zs[0][:quarter]
    incoming = jnp.where(z == 1, carried, jnp.zeros_like(carried))
    for place in (1, 2):
        carried = dot3(carried, zs[place][quarter:]) + zs[place][:quarter]
        incoming = jnp.where(z == place + 1, carried, incoming)
    through = jnp.where(x == 0, incoming, dot3(incoming, before[quarter:]) + before[:quarter])
    through = jnp.where(core == 0, through, dot3(through, even[quarter:]) + even[:quarter])
    started += spread(last_out, col, 4, "y", through)
    for copy in started:
        copy.wait_send()


def section_scan(solved, maps):
    rows, bs, width = solved.shape
    any_space = pl.BlockSpec(memory_space=pl.ANY)
    quarter = width // 4
    return pl.pallas_call(
        scan_kernel,
        out_shape=jax.ShapeDtypeStruct((4, quarter, bs), F32),
        in_specs=[any_space, any_space],
        out_specs=pl.BlockSpec(memory_space=pltpu.VMEM),
        scratch_shapes=[
            pltpu.VMEM((bs, width), F32),
            pltpu.VMEM((bs, bs), F32),
            pltpu.VMEM((4, quarter + bs, bs), F32),
            pltpu.VMEM((quarter + bs, bs), F32),
            pltpu.VMEM((quarter + bs, bs), F32),
            pltpu.VMEM((4, quarter + bs, bs), F32),
            pltpu.VMEM((4, quarter + bs, bs), F32),
            pltpu.SemaphoreType.DMA((2,)),
            pltpu.SemaphoreType.DMA((5, 4)),
            pltpu.SemaphoreType.DMA((5, 4)),
        ],
        compiler_params=pltpu.CompilerParams(collective_id=1, has_side_effects=True),
        name="section_scan",
    )(solved, maps)


def per_device(right_sides, diag_inverse, coupling, off_blocks, pattern):
    solved, maps = section_solve(right_sides[0, 0], diag_inverse[0, 0], coupling[0, 0], off_blocks[0, 0], pattern[0, 0])
    last = section_scan(solved, maps)
    last = last.reshape(-1, last.shape[-1])
    result = solved + jnp.einsum("pab,wb->paw", maps, last, precision=lax.Precision.HIGH)
    return result[None, None]


def solution(mesh):
    return jax.shard_map(
        per_device,
        mesh=mesh,
        in_specs=(
            P("sec", "col", None, None, None),
            P("sec", "col", None, None, None),
            P("sec", "col", None, None, None),
            P("sec", "col", None, None, None, None),
            P("sec", "col", None, None),
        ),
        out_specs=P("sec", "col", None, None, None),
        check_vma=False,
    )
```

```python
import functools

import jax
import jax.numpy as jnp
from jax import lax
from jax.experimental import pallas as pl
from jax.experimental.pallas import tpu as pltpu
from jax.sharding import PartitionSpec as P

LEV = 4
CHUNKS = 3
MESH = pl.DeviceIdType.MESH
F32 = jnp.float32
BF16 = jnp.bfloat16


def split(value):
    high = value.astype(BF16)
    return high, (value - high.astype(F32)).astype(BF16)


def dot(left, right):
    return jnp.dot(left, right, preferred_element_type=F32)


def dot3(left, right):
    left_high, left_low = split(left)
    right_high, right_low = split(right)
    both = dot(left_high, jnp.concatenate([right_high, right_low], axis=1))
    width = right.shape[1]
    return both[:, :width] + both[:, width:] + dot(left_low, right_high)


def dot_ready(left, high, low):
    left_high, left_low = split(left)
    return dot(left_high, high) + dot(left_high, low) + dot(left_low, high)


def section_kernel(
    pattern, right_sides, diag, coupling, off,
    y_out, w_out, last_out,
    rhs_v, diag_v, coup_v, off_v, got, table, top,
    maps, pairs, groups, lead, span_high, span_low, reach_high, reach_low, base, swapped, pair_base, begun, slices, sums, ends,
    in_sem, out_sem, send_sem, recv_sem, far_send, far_recv,
):
    me, sec = lax.axis_index("col"), lax.axis_index("sec")
    core = lax.rem(sec, 2)
    x = lax.rem(sec // 2, 4)
    z = sec // 8
    right, left, across = lax.rem(me + 1, 4), lax.rem(me + 3, 4), lax.rem(me + 2, 4)
    per_level = diag_v.shape[0] // LEV
    bs = diag_v.shape[1]
    half = per_level * bs // 2
    items = (LEV - 1) * CHUNKS
    last_k = per_level - 1
    piece = slices.shape[1]

    def at(x_step=0, y_step=0, z_step=0, swap=0):
        there = core + swap * (1 - 2 * core)
        return {
            "sec": (lax.rem(z + z_step, 4) * 4 + lax.rem(x + x_step, 4)) * 2 + there,
            "col": lax.rem(me + y_step, 4),
        }

    partners = [dict(x_step=i, y_step=j) for i in range(4) for j in range(4) if i or j]
    partners += [dict(z_step=i) for i in (1, 2, 3)]
    partners += [dict(y_step=j, swap=1) for j in range(4)]

    def level_rows(level):
        return pl.ds(level * per_level, per_level)

    loads = []
    for level in range(LEV):
        rows = level_rows(level)
        parts = [(coupling.at[rows], coup_v.at[rows]), (diag.at[rows], diag_v.at[rows]), (right_sides.at[rows], rhs_v.at[rows])]
        if level:
            lower = level_rows(level - 1)
            parts.append((off.at[lower], off_v.at[lower]))
        loads.append([pltpu.make_async_copy(a, b, in_sem.at[level, i]) for i, (a, b) in enumerate(parts)])
    for group in loads:
        for copy in group:
            copy.start()

    barrier = pltpu.get_barrier_semaphore()
    for partner in partners:
        pl.semaphore_signal(barrier, inc=1, device_id=at(**partner), device_id_type=MESH)


    lo, hi = pl.ds(0, half), pl.ds(half, half)

    def remote(item, slot, rows, index, target):
        ref = got.at[item, slot, rows]
        return pltpu.make_async_remote_copy(
            src_ref=ref, dst_ref=ref, send_sem=send_sem.at[item, index], recv_sem=recv_sem.at[item, index],
            device_id={"col": target}, device_id_type=MESH,
        )

    def own_sends(item):
        return [remote(item, me, lo, 0, right), remote(item, me, hi, 1, left), remote(item, me, hi, 2, right), remote(item, me, lo, 3, left)]

    def forwards(item):
        return [remote(item, left, lo, 4, right), remote(item, right, hi, 5, left)]

    def arrival(item, index):
        slot = (left, right, left, right, across, across)[index]
        return remote(item, slot, (lo, hi, hi, lo, lo, hi)[index], index, right)

    def forward(item):
        arrival(item, 0).wait_recv()
        go = forwards(item)
        go[0].start()
        arrival(item, 1).wait_recv()
        go[1].start()

    def finish(item):
        for index in range(2, 6):
            arrival(item, index).wait_recv()

    def to_table(level, chunk):
        item = level * CHUNKS + chunk
        first = chunk * (LEV - 1) * 4 * per_level + level * 4 * per_level

        def body(k, carry):
            for source in range(4):
                high, low = split(got[item, source, pl.ds(pl.multiple_of(k * bs, bs), bs), :])
                table[first + source * per_level + k, :, :bs] = high
                table[first + source * per_level + k, :, bs:] = low
            return carry

        lax.fori_loop(0, per_level, body, 0)

    def compute(level, chunk, start=0, stop=None):
        def body(k, carry):
            row = level * per_level + k
            if chunk == 0:
                current = -coup_v[row]
            else:
                current = rhs_v[row, :, (chunk - 1) * bs : chunk * bs]
            if level:
                low_row = (level - 1) * per_level + k
                wide = jnp.zeros((bs, 2 * bs), F32)
                narrow = jnp.zeros((bs, bs), F32)
                first = chunk * (LEV - 1) * 4 * per_level
                for begin in range(0, 16, 4):
                    pieces = [split(off_v[low_row, j]) for j in range(begin, begin + 4)]
                    picked = jnp.concatenate([table[first + pattern[low_row, 0, j]] for j in range(begin, begin + 4)], axis=0)
                    wide += dot(jnp.concatenate([p[0] for p in pieces], axis=1), picked)
                    narrow += dot(jnp.concatenate([p[1] for p in pieces], axis=1), picked[:, :bs])
                current = current - (wide[:, :bs] + wide[:, bs:] + narrow)
            solved = dot3(diag_v[row], current)
            if level < LEV - 1:
                got[level * CHUNKS + chunk, me, pl.ds(pl.multiple_of(k * bs, bs), bs), :] = solved
            else:
                top[chunk, pl.ds(pl.multiple_of(k * bs, bs), bs), :] = solved
            return carry

        lax.fori_loop(start, per_level if stop is None else stop, body, 0)

    def writes(level, chunk):
        source = got.at[level * CHUNKS + chunk, me] if level < LEV - 1 else top.at[chunk]
        copies = []
        for k in range(per_level):
            row = level * per_level + k
            target = w_out.at[row] if chunk == 0 else y_out.at[row, :, pl.ds((chunk - 1) * bs, bs)]
            copies.append(pltpu.make_async_copy(source.at[pl.ds(k * bs, bs)], target, out_sem.at[level * CHUNKS + chunk, k]))
        return copies


    def far(source, target, phase, index, own_index=None, **step):
        return pltpu.make_async_remote_copy(
            src_ref=source, dst_ref=target,
            send_sem=far_send.at[phase, index if own_index is None else own_index], recv_sem=far_recv.at[phase, index],
            device_id=at(**step), device_id_type=MESH,
        )

    boundary = me == LEV - 1
    last_rows = pl.ds(last_k * bs, bs)
    mine = core * 4 + me
    map_swap = far(maps.at[core], maps.at[core], 0, 0, swap=1)
    pair_down = [far(pairs.at[x], pairs.at[x], 1, j, y_step=j) for j in (1, 2, 3)]
    map_down = [far(maps.at[0], maps.at[0], 1, j, y_step=j) for j in (1, 2, 3)]
    pair_swap = far(pairs.at[x], pairs.at[x], 2, 0, swap=1)
    even_swap = far(maps.at[0], maps.at[0], 2, 1, swap=1)
    pair_round = [far(pairs.at[x], pairs.at[x], 3, j, x_step=j) for j in (1, 2, 3)]
    group_round = [far(groups.at[z], groups.at[z], 4, j, z_step=j) for j in (1, 2, 3)]
    base_swap = far(base.at[1 - core], swapped, 5, 0, swap=1)
    pair_spread = {
        (i, q): far(pair_base.at[q], slices.at[x], 6, i, i * 4 + q, x_step=i, y_step=q + 1)
        for i in range(4) for q in range(4) if i or q < 3
    }
    begun_spread = [far(begun.at[q], begun.at[q], 7, 0, q, y_step=q + 1) for q in range(3)]
    sum_round = [far(sums.at[z], sums.at[z], 8, j, z_step=j) for j in (1, 2, 3)]
    end_round = [
        far(ends.at[core + s * (1 - 2 * core)], last_out.at[mine], 9, j * 2 + s, y_step=j, swap=s)
        for j in range(4) for s in range(2) if j or s
    ]
    eye = (lax.broadcasted_iota(jnp.int32, (bs, bs), 0) == lax.broadcasted_iota(jnp.int32, (bs, bs), 1)).astype(F32)
    nothing = jnp.zeros((bs, bs), F32)

    def start_all(copies):
        for copy in copies:
            copy.start()

    def maps_swap():
        @pl.when(boundary)
        def _():
            maps[core] = top[0, last_rows].T
            map_swap.start()

    def maps_down():
        @pl.when(boundary)
        def _():
            map_swap.wait()
            pairs[x] = dot3(maps[0], maps[1])

            @pl.when(core == 0)
            def _():
                start_all(pair_down)

            @pl.when(core == 1)
            def _():
                start_all(map_down)

    def maps_join():
        for part in range(3):

            @pl.when(me == part)
            def _(part=part):
                @pl.when(core == 0)
                def _():
                    pair_down[part].wait_recv()
                    pair_swap.start()

                @pl.when(core == 1)
                def _():
                    map_down[part].wait_recv()
                    even_swap.start()

    def maps_round():
        @pl.when(jnp.logical_not(boundary))
        def _():
            @pl.when(core == 0)
            def _():
                pair_swap.wait_send()
                even_swap.wait_recv()

            @pl.when(core == 1)
            def _():
                even_swap.wait_send()
                pair_swap.wait_recv()

        start_all(pair_round)

    def maps_products():
        for copy in pair_round:
            copy.wait_recv()
        after = [None, None, pairs[3], eye]
        after[1] = dot3(pairs[2], pairs[3])
        after[0] = dot3(pairs[1], after[1])
        groups[z] = dot3(pairs[0], after[0])
        start_all(group_round)
        inside = [None, None, jnp.where(x == 3, eye, nothing), nothing]
        for i in (1, 0):
            inside[i] = jnp.where(x == i + 1, eye, dot3(pairs[i + 1], inside[i + 1]))
        lead[...] = jnp.where(x == 0, eye, dot3(pairs[0], inside[0]))
        for i in range(4):
            for j, value in enumerate((after[i], inside[i])):
                high, low = split(value)
                span_high[i * bs : (i + 1) * bs, j * bs : (j + 1) * bs] = high
                span_low[i * bs : (i + 1) * bs, j * bs : (j + 1) * bs] = low

    def maps_reach():
        for copy in group_round:
            copy.wait_recv()
        inside = [None, None, jnp.where(z == 3, lead[...], nothing), nothing]
        for i in (1, 0):
            inside[i] = jnp.where(z == i + 1, lead[...], dot3(groups[i + 1], inside[i + 1]))
        for i in range(4):
            high, low = split(inside[i])
            reach_high[i * bs : (i + 1) * bs, :] = high
            reach_low[i * bs : (i + 1) * bs, :] = low

    def base_start():
        @pl.when(boundary)
        def _():
            for part in range(2):
                base[part] = top[part + 1, last_rows].T
            base_swap.start()

    def base_share():
        @pl.when(boundary)
        def _():
            base_swap.wait()
            own, other = base[core], swapped[...]
            even = jnp.where(core == 0, own, other)
            odd = jnp.where(core == 0, other, own)
            both = dot3(even, maps[1]) + odd
            for q in range(4):
                pair_base[q] = both[q * piece : (q + 1) * piece]
                begun[q] = even[q * piece : (q + 1) * piece]
            start_all(pair_spread.values())
            start_all(begun_spread)
            slices[x] = pair_base[3]

    def sums_start():
        @pl.when(jnp.logical_not(boundary))
        def _():
            pair_spread[0, 0].wait_recv()

        for i in (1, 2, 3):
            pair_spread[i, 0].wait_recv()
        joined = jnp.concatenate([slices[i] for i in range(4)], axis=1)
        both = dot_ready(joined, span_high[...], span_low[...])
        sums[z] = both[:, :bs]
        start_all(sum_round)
        return both[:, bs:]

    def ends_start(inside):
        for copy in sum_round:
            copy.wait_recv()
        joined = jnp.concatenate([sums[i] for i in range(4)], axis=1)
        enter = inside + dot_ready(joined, reach_high[...], reach_low[...])

        @pl.when(jnp.logical_not(boundary))
        def _():
            begun_spread[0].wait_recv()

        ends[0] = enter
        ends[1] = begun[me] + dot3(enter, maps[0])
        last_out[mine] = ends[core]
        start_all(end_round)

    def scan_sends_end():
        @pl.when(boundary)
        def _():
            @pl.when(core == 0)
            def _():
                for copy in pair_down:
                    copy.wait_send()

            @pl.when(core == 1)
            def _():
                for copy in map_down:
                    copy.wait_send()

            for copy in list(pair_spread.values()) + begun_spread:
                copy.wait_send()

        for copy in pair_round + group_round + sum_round + end_round:
            copy.wait_send()

    for copy in loads[0]:
        copy.wait()
    compute(0, 0)
    pl.semaphore_wait(barrier, len(partners))
    top_level = LEV - 1
    for item in range(items):
        start_all(own_sends(item))
        start_all(writes(item // CHUNKS, item % CHUNKS))
        following = item + 1
        if following < items:
            level, chunk = following // CHUNKS, following % CHUNKS
            if level:
                if chunk == 0:
                    for copy in loads[level]:
                        copy.wait()
                finish(following - CHUNKS)
                to_table(level - 1, chunk)
            compute(level, chunk)
        if item == items - 2:
            for copy in loads[top_level]:
                copy.wait()
            finish(items - 3)
            to_table(top_level - 1, 0)
            compute(top_level, 0, last_k)
            maps_swap()
            compute(top_level, 0, 0, last_k)
            maps_down()
        if item == items - 1:
            start_all(writes(top_level, 0))
            finish(items - 2)
            to_table(top_level - 1, 1)
            maps_join()
            compute(top_level, 1, last_k)
            maps_round()
            compute(top_level, 1, 0, last_k)
        forward(item)
    start_all(writes(top_level, 1))
    maps_products()
    finish(items - 1)
    to_table(top_level - 1, 2)
    compute(top_level, 2, last_k)
    base_start()
    maps_reach()
    base_share()
    compute(top_level, 2, 0, last_k)
    start_all(writes(top_level, 2))
    inside = sums_start()
    ends_start(inside)
    for item in range(items):
        for copy in own_sends(item) + forwards(item):
            copy.wait_send()
    for item in range(LEV * CHUNKS):
        for copy in writes(item // CHUNKS, item % CHUNKS):
            copy.wait()
    for copy in end_round:
        copy.wait_recv()
    scan_sends_end()


def section_solve(right_sides, diag_inverse, coupling, off_blocks, pattern):
    rows, bs, width = right_sides.shape
    per_level = rows // LEV
    items = (LEV - 1) * CHUNKS
    any_space = pl.BlockSpec(memory_space=pl.ANY)
    piece = width // 8
    return pl.pallas_call(
        section_kernel,
        out_shape=(
            jax.ShapeDtypeStruct((rows, bs, width), F32),
            jax.ShapeDtypeStruct((rows, bs, bs), F32),
            jax.ShapeDtypeStruct((8, piece, bs), F32),
        ),
        in_specs=[pl.BlockSpec(memory_space=pltpu.SMEM)] + [any_space] * 4,
        out_specs=(any_space, any_space, pl.BlockSpec(memory_space=pltpu.VMEM)),
        scratch_shapes=[
            pltpu.VMEM((rows, bs, width), F32),
            pltpu.VMEM((rows, bs, bs), F32),
            pltpu.VMEM((rows, bs, bs), F32),
            pltpu.VMEM(off_blocks.shape, F32),
            pltpu.VMEM((items, 4, per_level * bs, bs), F32),
            pltpu.VMEM((CHUNKS * (LEV - 1) * 4 * per_level, bs, 2 * bs), BF16),
            pltpu.VMEM((CHUNKS, per_level * bs, bs), F32),
            pltpu.VMEM((2, bs, bs), F32),
            pltpu.VMEM((4, bs, bs), F32),
            pltpu.VMEM((4, bs, bs), F32),
            pltpu.VMEM((bs, bs), F32),
            pltpu.VMEM((4 * bs, 2 * bs), BF16),
            pltpu.VMEM((4 * bs, 2 * bs), BF16),
            pltpu.VMEM((4 * bs, bs), BF16),
            pltpu.VMEM((4 * bs, bs), BF16),
            pltpu.VMEM((2, bs, bs), F32),
            pltpu.VMEM((bs, bs), F32),
            pltpu.VMEM((4, piece, bs), F32),
            pltpu.VMEM((4, piece, bs), F32),
            pltpu.VMEM((4, piece, bs), F32),
            pltpu.VMEM((4, piece, bs), F32),
            pltpu.VMEM((2, piece, bs), F32),
            pltpu.SemaphoreType.DMA((LEV, 4)),
            pltpu.SemaphoreType.DMA((LEV * CHUNKS, per_level)),
            pltpu.SemaphoreType.DMA((items, 6)),
            pltpu.SemaphoreType.DMA((items, 6)),
            pltpu.SemaphoreType.DMA((10, 16)),
            pltpu.SemaphoreType.DMA((10, 16)),
        ],
        compiler_params=pltpu.CompilerParams(collective_id=0, has_side_effects=True, vmem_limit_bytes=58 << 20),
        name="section_solve",
    )(pattern.reshape(pattern.shape[0], 1, pattern.shape[1]), right_sides, diag_inverse, coupling, off_blocks)


def per_device(right_sides, diag_inverse, coupling, off_blocks, pattern):
    solved, maps, last = section_solve(right_sides[0, 0], diag_inverse[0, 0], coupling[0, 0], off_blocks[0, 0], pattern[0, 0])
    last = last.reshape(-1, last.shape[-1])
    result = solved + jnp.einsum("pab,wb->paw", maps, last, precision=lax.Precision.HIGH)
    return result[None, None]


def solution(mesh):
    return jax.shard_map(
        per_device,
        mesh=mesh,
        in_specs=(
            P("sec", "col", None, None, None),
            P("sec", "col", None, None, None),
            P("sec", "col", None, None, None),
            P("sec", "col", None, None, None, None),
            P("sec", "col", None, None),
        ),
        out_specs=P("sec", "col", None, None, None),
        check_vma=False,
    )
```

```python
import functools

import jax
import jax.numpy as jnp
from jax import lax
from jax.experimental import pallas as pl
from jax.experimental.pallas import tpu as pltpu
from jax.sharding import PartitionSpec as P

LEV = 4
CHUNKS = 3
SHIFTED = (1, 2, 3)
MESH = pl.DeviceIdType.MESH
F32 = jnp.float32
BF16 = jnp.bfloat16


def split(value):
    high = value.astype(BF16)
    return high, (value - high.astype(F32)).astype(BF16)


def dot(left, right):
    return jnp.dot(left, right, preferred_element_type=F32)


def dot3(left, right):
    left_high, left_low = split(left)
    right_high, right_low = split(right)
    both = dot(left_high, jnp.concatenate([right_high, right_low], axis=1))
    width = right.shape[1]
    return both[:, :width] + both[:, width:] + dot(left_low, right_high)


def dot_ready(left, high, low):
    left_high, left_low = split(left)
    return dot(left_high, high) + dot(left_high, low) + dot(left_low, high)


def section_kernel(
    pattern, right_sides, diag, coupling, off,
    out,
    rhs_v, diag_v, coup_v, off_v, got, table, top,
    z_made, z_here, share, map_cut, map_parts, maps, pairs, groups, lead,
    span_high, span_low, reach_high, reach_low,
    base_cut, base_parts, begun, slices, sums, ends, entered, enter_high, enter_low,
    in_sem, out_sem, send_sem, recv_sem, far_send, far_recv,
):
    me, sec = lax.axis_index("col"), lax.axis_index("sec")
    core = lax.rem(sec, 2)
    x = lax.rem(sec // 2, 4)
    z = sec // 8
    right, left, across = lax.rem(me + 1, 4), lax.rem(me + 3, 4), lax.rem(me + 2, 4)
    boundary = me == 3
    per_level = diag_v.shape[0] // LEV
    bs = diag_v.shape[1]
    items = (LEV - 1) * CHUNKS
    last_row = LEV * per_level - 1
    last_low = (LEV - 1) * per_level - 1
    below = (LEV - 2) * 4 * per_level
    positions = (LEV - 1) * 4 * per_level
    piece = slices.shape[1]

    def start_all(copies):
        for copy in copies:
            copy.start()

    def at(x_step=0, y_step=0, z_step=0, to_core=None):
        there = core if to_core is None else to_core
        return {
            "sec": (lax.rem(z + z_step, 4) * 4 + lax.rem(x + x_step, 4)) * 2 + there,
            "col": lax.rem(me + y_step, 4),
        }

    partners = [dict(x_step=i) for i in (1, 2, 3)] + [dict(z_step=i) for i in (1, 2, 3)]
    partners += [dict(y_step=j) for j in (1, 2, 3)] + [dict(y_step=j, to_core=1 - core) for j in range(4)]

    def level_rows(level):
        return pl.ds(level * per_level, per_level)

    loads = []
    for level in range(LEV):
        rows = level_rows(level)
        parts = [(coupling.at[rows], coup_v.at[rows]), (diag.at[rows], diag_v.at[rows]), (right_sides.at[rows], rhs_v.at[rows])]
        if level:
            lower = level_rows(level - 1)
            parts.append((off.at[lower], off_v.at[lower]))
        loads.append([pltpu.make_async_copy(a, b, in_sem.at[level, i]) for i, (a, b) in enumerate(parts)])
    start_all(loads[0])

    barrier = pltpu.get_barrier_semaphore()
    for partner in partners:
        pl.semaphore_signal(barrier, inc=1, device_id=at(**partner), device_id_type=MESH)


    def count_of(item):
        return 4 if item in SHIFTED else 2

    def ring(item, slot, p, index, target, own_index=None):
        size = per_level * bs // count_of(item)
        ref = got.at[item, slot, pl.ds(p * size, size)]
        return pltpu.make_async_remote_copy(
            src_ref=ref, dst_ref=ref,
            send_sem=send_sem.at[item, index if own_index is None else own_index], recv_sem=recv_sem.at[item, index],
            device_id={"col": target}, device_id_type=MESH,
        )

    def own_sends(item):
        count = count_of(item)
        copies = []
        for p in range(count):
            copies.append(ring(item, me, p, p, right))
            copies.append(ring(item, me, count - 1 - p, 4 + count - 1 - p, left))
        return copies

    def from_left(item, p):
        return ring(item, left, p, p, right)

    def from_right(item, p):
        return ring(item, right, p, 4 + p, right)

    def to_right(item, p):
        return ring(item, left, p, 8 + p, right)

    def to_left(item, p):
        return ring(item, right, p, 8 + p, left, 12 + p)

    def forward_steps(item):
        if count_of(item) == 2:
            return [(0, True, None), (1, False, None)]
        return [
            (0, True, None), (3, False, None),
            (1, True, left != 2), (2, False, right != 0),
            (2, True, left == 0), (1, False, right == 2),
        ]

    def forward(item):
        for p, rightward, allowed in forward_steps(item):
            (from_left if rightward else from_right)(item, p).wait_recv()
            go = (to_right if rightward else to_left)(item, p)
            if allowed is None:
                go.start()
            else:
                pl.when(allowed)(go.start)

    def finish(item):
        count = count_of(item)
        from_left(item, count - 1).wait_recv()
        from_right(item, 0).wait_recv()
        for p in range(count):
            ring(item, across, p, 8 + p, right).wait_recv()

    def ring_sends_end(item):
        for copy in own_sends(item):
            copy.wait_send()
        for p, rightward, allowed in forward_steps(item):
            gone = (to_right if rightward else to_left)(item, p)
            if allowed is None:
                gone.wait_send()
            else:
                pl.when(allowed)(gone.wait_send)

    def to_table(level, chunk):
        item = level * CHUNKS + chunk
        first = chunk * positions + level * 4 * per_level

        def body(k, carry):
            for source in range(4):
                high, low = split(got[item, source, pl.ds(pl.multiple_of(k * bs, bs), bs), :])
                table[first + source * per_level + k, :, :bs] = high
                table[first + source * per_level + k, :, bs:] = low
            return carry

        lax.fori_loop(0, per_level, body, 0)

    def reduced(row, low_row, chunk, limit=None):
        if chunk == 0:
            current = -coup_v[row]
        else:
            current = rhs_v[row, :, (chunk - 1) * bs : chunk * bs]
        if low_row is None:
            return current
        wide = jnp.zeros((bs, 2 * bs), F32)
        narrow = jnp.zeros((bs, bs), F32)
        for begin in range(0, 16, 4):
            pieces = [split(off_v[low_row, j]) for j in range(begin, begin + 4)]
            places = [pattern[low_row, 0, j] for j in range(begin, begin + 4)]
            if limit is None:
                places = [chunk * positions + place for place in places]
            else:
                places = [jnp.where(place < limit, chunk * positions + place, CHUNKS * positions) for place in places]
            picked = jnp.concatenate([table[place] for place in places], axis=0)
            wide += dot(jnp.concatenate([p[0] for p in pieces], axis=1), picked)
            narrow += dot(jnp.concatenate([p[1] for p in pieces], axis=1), picked[:, :bs])
        return current - (wide[:, :bs] + wide[:, bs:] + narrow)

    def compute(level, chunk):
        def body(k, carry):
            row = level * per_level + k
            solved = dot3(diag_v[row], reduced(row, (level - 1) * per_level + k if level else None, chunk))
            if level < LEV - 1:
                got[level * CHUNKS + chunk, me, pl.ds(pl.multiple_of(k * bs, bs), bs), :] = solved
            else:
                top[chunk, pl.ds(pl.multiple_of(k * bs, bs), bs), :] = solved
            return carry

        lax.fori_loop(0, per_level, body, 0)


    def z_copy(owner, k):
        return pltpu.make_async_remote_copy(
            src_ref=z_made.at[owner, k], dst_ref=z_here.at[k], send_sem=far_send.at[0, owner * per_level + k],
            recv_sem=far_recv.at[0, k], device_id=at(y_step=owner + 1), device_id_type=MESH,
        )

    def z_make(begin, end):
        @pl.when(boundary)
        def _():
            def body(step, carry):
                k, owner = begin + step // 4, lax.rem(step, 4)
                place = below + owner * per_level + k
                which, found = jnp.int32(0), jnp.int32(0)
                for j in range(16):
                    same = (pattern[last_low, 0, j] == place).astype(jnp.int32)
                    which, found = which + j * same, found + same
                block = dot3(diag_v[last_row], off_v[last_low, which])
                z_made[owner, k] = jnp.where(found > 0, -block, jnp.zeros_like(block))
                return carry

            lax.fori_loop(0, 4 * (end - begin), body, 0)
            for k in range(begin, end):
                start_all([z_copy(owner, k) for owner in range(3)])
                z_here[k] = z_made[3, k]

    def z_wait():
        @pl.when(jnp.logical_not(boundary))
        def _():
            for k in range(per_level):
                z_copy(0, k).wait_recv()

    def shared(chunk):
        left_side = jnp.concatenate([z_here[k] for k in range(per_level)], axis=1)
        share[...] = dot3(left_side, got[(LEV - 2) * CHUNKS + chunk, me])

        @pl.when(boundary)
        def _():
            share[...] += dot3(diag_v[last_row], reduced(last_row, last_low, chunk, below))

        return share[...].T


    def far(source, target, phase, index, own_index=None, **step):
        return pltpu.make_async_remote_copy(
            src_ref=source, dst_ref=target,
            send_sem=far_send.at[phase, index if own_index is None else own_index], recv_sem=far_recv.at[phase, index],
            device_id=at(**step), device_id_type=MESH,
        )

    def map_of(which):
        return maps[which].reshape(bs, bs)

    rounds = (1, 2, 3)
    other = 1 - core
    map_scatter = [far(map_cut.at[lax.rem(me + j, 4)], map_parts.at[me], 1, j, y_step=j) for j in rounds]
    map_gather = [far(maps.at[core, me], maps.at[core, me], 2, j, y_step=j) for j in rounds]
    map_swap = far(maps.at[core], maps.at[core], 2, 4, to_core=other)
    pair_round = [far(pairs.at[x], pairs.at[x], 3, j, x_step=j) for j in rounds]
    group_round = [far(groups.at[z], groups.at[z], 4, j, z_step=j) for j in rounds]
    base_scatter = [
        [
            far(base_cut.at[h, lax.rem(me + j, 4)], base_parts.at[core, me], 5 + h, j * 2 + core, j, y_step=j, to_core=h)
            for j in range(4)
        ]
        for h in range(2)
    ]
    slice_round = [far(slices.at[x], slices.at[x], 7, j, x_step=j) for j in rounds]
    sum_round = [far(sums.at[z], sums.at[z], 8, j, z_step=j) for j in rounds]
    mine = core * 4 + me
    end_round = [
        far(ends.at[core if s == 0 else other], entered.at[mine], 9, j * 2 + s, y_step=j, to_core=core if s == 0 else other)
        for j in range(4) for s in range(2) if j or s
    ]
    eye = (lax.broadcasted_iota(jnp.int32, (bs, bs), 0) == lax.broadcasted_iota(jnp.int32, (bs, bs), 1)).astype(F32)
    nothing = jnp.zeros((bs, bs), F32)

    def wait_all(copies):
        for copy in copies:
            copy.wait_recv()

    def maps_scatter():
        value = shared(0)
        for q in range(4):
            map_cut[q] = value[q * piece : (q + 1) * piece]
        start_all(map_scatter)
        map_parts[me] = map_cut[me]

    def maps_gather():
        wait_all(map_scatter)
        maps[core, me] = (map_parts[0] + map_parts[1]) + (map_parts[2] + map_parts[3])
        start_all(map_gather)

    def maps_swap():
        wait_all(map_gather)
        map_swap.start()

    def maps_round():
        map_swap.wait_recv()
        pairs[x] = dot3(map_of(0), map_of(1))
        start_all(pair_round)

    def maps_products():
        wait_all(pair_round)
        after = [None, None, pairs[3], eye]
        after[1] = dot3(pairs[2], pairs[3])
        after[0] = dot3(pairs[1], after[1])
        groups[z] = dot3(pairs[0], after[0])
        start_all(group_round)
        inside = [None, None, jnp.where(x == 3, eye, nothing), nothing]
        for i in (1, 0):
            inside[i] = jnp.where(x == i + 1, eye, dot3(pairs[i + 1], inside[i + 1]))
        lead[...] = jnp.where(x == 0, eye, dot3(pairs[0], inside[0]))
        for i in range(4):
            for j, value in enumerate((after[i], inside[i])):
                high, low = split(value)
                span_high[i * bs : (i + 1) * bs, j * bs : (j + 1) * bs] = high
                span_low[i * bs : (i + 1) * bs, j * bs : (j + 1) * bs] = low

    def maps_reach():
        wait_all(group_round)
        inside = [None, None, jnp.where(z == 3, lead[...], nothing), nothing]
        for i in (1, 0):
            inside[i] = jnp.where(z == i + 1, lead[...], dot3(groups[i + 1], inside[i + 1]))
        for i in range(4):
            high, low = split(inside[i])
            reach_high[i * bs : (i + 1) * bs, :] = high
            reach_low[i * bs : (i + 1) * bs, :] = low

    def bases_scatter(chunk):
        h = chunk - 1
        value = shared(chunk)
        for q in range(4):
            base_cut[h, q] = value[q * piece : (q + 1) * piece]
        start_all(base_scatter[h][1:])

        @pl.when(core != h)
        def _():
            base_scatter[h][0].start()

        @pl.when(core == h)
        def _():
            base_parts[core, me] = base_cut[h, me]

    def slices_start():
        for h in range(2):

            @pl.when(core == h)
            def _(h=h):
                for j in range(4):
                    for source in range(2):
                        if j or source != h:
                            far(base_cut.at[h, 0], base_parts.at[source, lax.rem(me + 4 - j, 4)], 5 + h, j * 2 + source, j).wait_recv()

        even = (base_parts[0, 0] + base_parts[0, 1]) + (base_parts[0, 2] + base_parts[0, 3])
        odd = (base_parts[1, 0] + base_parts[1, 1]) + (base_parts[1, 2] + base_parts[1, 3])
        begun[...] = even
        slices[x] = dot3(even, map_of(1)) + odd
        start_all(slice_round)

    def sums_start():
        wait_all(slice_round)
        joined = jnp.concatenate([slices[i] for i in range(4)], axis=1)
        both = dot_ready(joined, span_high[...], span_low[...])
        sums[z] = both[:, :bs]
        start_all(sum_round)
        ends[0] = both[:, bs:]

    def ends_start():
        wait_all(sum_round)
        joined = jnp.concatenate([sums[i] for i in range(4)], axis=1)
        enter = ends[0] + dot_ready(joined, reach_high[...], reach_low[...])
        ends[0] = enter
        ends[1] = begun[...] + dot3(enter, map_of(0))
        entered[mine] = ends[core]
        start_all(end_round)

    def scan_sends_end():
        @pl.when(boundary)
        def _():
            for k in range(per_level):
                for owner in range(3):
                    z_copy(owner, k).wait_send()

        for h in range(2):
            for copy in base_scatter[h][1:]:
                copy.wait_send()

            @pl.when(core != h)
            def _(h=h):
                base_scatter[h][0].wait_send()

        for copy in map_scatter + map_gather + [map_swap] + pair_round + group_round + slice_round + sum_round + end_round:
            copy.wait_send()


    def enter():
        wait_all(end_round)
        for h in range(2):
            value = jnp.concatenate([entered[h * 4 + q] for q in range(4)], axis=0).T
            high, low = split(value)
            enter_high[:, h * bs : (h + 1) * bs] = high
            enter_low[:, h * bs : (h + 1) * bs] = low

    def correct(level):
        def body(k, carry):
            rows = pl.ds(pl.multiple_of(k * bs, bs), bs)
            if level < LEV - 1:
                parts = [got[level * CHUNKS + chunk, me, rows, :] for chunk in range(CHUNKS)]
            else:
                parts = [top[chunk, rows, :] for chunk in range(CHUNKS)]
            change = dot_ready(parts[0], enter_high[...], enter_low[...])
            for h in range(2):
                rhs_v[level * per_level + k, :, h * bs : (h + 1) * bs] = parts[1 + h] + change[:, h * bs : (h + 1) * bs]
            return carry

        lax.fori_loop(0, per_level, body, 0)
        writes[level].start()

    writes = [pltpu.make_async_copy(rhs_v.at[level_rows(level)], out.at[level_rows(level)], out_sem.at[level]) for level in range(LEV)]

    top_level = LEV - 1
    table[CHUNKS * positions] = jnp.zeros((bs, 2 * bs), BF16)
    for copy in loads[0]:
        copy.wait()
    for group in loads[1:]:
        start_all(group)
    compute(0, 0)
    pl.semaphore_wait(barrier, len(partners))
    for item in range(items):
        start_all(own_sends(item))
        following = item + 1
        if following < items - 1:
            level, chunk = following // CHUNKS, following % CHUNKS
            if level:
                finish(following - CHUNKS)
                to_table(level - 1, chunk)
            compute(level, chunk)
        if item == 1:
            for group in loads[1:]:
                for copy in group:
                    copy.wait()
        if item in (1, 2, 3):
            z_make(2 * item - 2, min(2 * item, per_level))
        if item == 5:
            z_wait()
            maps_scatter()
        if item == 6:
            maps_gather()
            bases_scatter(1)
            finish(5)
            to_table(1, 2)
            compute(2, 2)
            bases_scatter(2)
            maps_swap()
        if item == 7:
            maps_round()
            finish(6)
            to_table(2, 0)
            compute(3, 0)
        if item == 8:
            slices_start()
            maps_products()
            finish(7)
            to_table(2, 1)
            sums_start()
            maps_reach()
            compute(3, 1)
            ends_start()
        forward(item)
    finish(items - 1)
    to_table(2, 2)
    compute(3, 2)
    enter()
    for level in reversed(range(LEV)):
        correct(level)
    for item in range(items):
        ring_sends_end(item)
    scan_sends_end()
    for copy in writes:
        copy.wait()


def section_solve(right_sides, diag_inverse, coupling, off_blocks, pattern):
    rows, bs, width = right_sides.shape
    per_level = rows // LEV
    items = (LEV - 1) * CHUNKS
    any_space = pl.BlockSpec(memory_space=pl.ANY)
    piece = width // 8
    full = pltpu.VMEM((bs, bs), F32)
    four = pltpu.VMEM((4, bs, bs), F32)
    cut = pltpu.VMEM((4, piece, bs), F32)
    cuts = pltpu.VMEM((2, 4, piece, bs), F32)
    return pl.pallas_call(
        section_kernel,
        out_shape=jax.ShapeDtypeStruct((rows, bs, width), F32),
        in_specs=[pl.BlockSpec(memory_space=pltpu.SMEM)] + [any_space] * 4,
        out_specs=any_space,
        scratch_shapes=[
            pltpu.VMEM((rows, bs, width), F32),
            pltpu.VMEM((rows, bs, bs), F32),
            pltpu.VMEM((rows, bs, bs), F32),
            pltpu.VMEM(off_blocks.shape, F32),
            pltpu.VMEM((items, 4, per_level * bs, bs), F32),
            pltpu.VMEM((CHUNKS * (LEV - 1) * 4 * per_level + 1, bs, 2 * bs), BF16),
            pltpu.VMEM((CHUNKS, per_level * bs, bs), F32),
            pltpu.VMEM((4, per_level, bs, bs), F32),
            pltpu.VMEM((per_level, bs, bs), F32),
            full,
            cut, cut, cuts, four, four, full,
            pltpu.VMEM((4 * bs, 2 * bs), BF16),
            pltpu.VMEM((4 * bs, 2 * bs), BF16),
            pltpu.VMEM((4 * bs, bs), BF16),
            pltpu.VMEM((4 * bs, bs), BF16),
            cuts, cuts,
            pltpu.VMEM((piece, bs), F32),
            cut, cut,
            pltpu.VMEM((2, piece, bs), F32),
            pltpu.VMEM((8, piece, bs), F32),
            pltpu.VMEM((bs, width), BF16),
            pltpu.VMEM((bs, width), BF16),
            pltpu.SemaphoreType.DMA((LEV, 4)),
            pltpu.SemaphoreType.DMA((LEV,)),
            pltpu.SemaphoreType.DMA((items, 16)),
            pltpu.SemaphoreType.DMA((items, 12)),
            pltpu.SemaphoreType.DMA((10, 16)),
            pltpu.SemaphoreType.DMA((10, 16)),
        ],
        compiler_params=pltpu.CompilerParams(collective_id=0, has_side_effects=True, vmem_limit_bytes=58 << 20),
        name="section_solve",
    )(pattern.reshape(pattern.shape[0], 1, pattern.shape[1]), right_sides, diag_inverse, coupling, off_blocks)


def per_device(right_sides, diag_inverse, coupling, off_blocks, pattern):
    result = section_solve(right_sides[0, 0], diag_inverse[0, 0], coupling[0, 0], off_blocks[0, 0], pattern[0, 0])
    return result[None, None]


def solution(mesh):
    return jax.shard_map(
        per_device,
        mesh=mesh,
        in_specs=(
            P("sec", "col", None, None, None),
            P("sec", "col", None, None, None),
            P("sec", "col", None, None, None),
            P("sec", "col", None, None, None, None),
            P("sec", "col", None, None),
        ),
        out_specs=P("sec", "col", None, None, None),
        check_vma=False,
    )
```

```python
import functools

import jax
import jax.numpy as jnp
from jax import lax
from jax.experimental import pallas as pl
from jax.experimental.pallas import tpu as pltpu
from jax.sharding import PartitionSpec as P

LEV = 4
CHUNKS = 3
SHIFTED = (1, 2, 3)
MESH = pl.DeviceIdType.MESH
F32 = jnp.float32
BF16 = jnp.bfloat16


def split(value):
    high = value.astype(BF16)
    return high, (value - high.astype(F32)).astype(BF16)


def dot(left, right):
    return jnp.dot(left, right, preferred_element_type=F32)


def dot3(left, right):
    left_high, left_low = split(left)
    right_high, right_low = split(right)
    both = dot(left_high, jnp.concatenate([right_high, right_low], axis=1))
    width = right.shape[1]
    return both[:, :width] + both[:, width:] + dot(left_low, right_high)


def dot_ready(left, high, low):
    left_high, left_low = split(left)
    return dot(left_high, high) + dot(left_high, low) + dot(left_low, high)


def section_kernel(
    pattern, right_sides, diag, coupling, off,
    out,
    rhs_v, diag_v, coup_v, off_v, got, table, top,
    z_made, z_here, share, map_cut, map_parts, maps, pairs, groups, lead,
    span_high, span_low, reach_high, reach_low,
    base_cut, base_parts, begun, slices, sums, ends, entered, enter_high, enter_low,
    in_sem, out_sem, send_sem, recv_sem, far_send, far_recv,
):
    me, sec = lax.axis_index("col"), lax.axis_index("sec")
    core = lax.rem(sec, 2)
    x = lax.rem(sec // 2, 4)
    z = sec // 8
    right, left, across = lax.rem(me + 1, 4), lax.rem(me + 3, 4), lax.rem(me + 2, 4)
    boundary = me == 3
    per_level = diag_v.shape[0] // LEV
    bs = diag_v.shape[1]
    items = (LEV - 1) * CHUNKS
    last_row = LEV * per_level - 1
    last_low = (LEV - 1) * per_level - 1
    below = (LEV - 2) * 4 * per_level
    positions = (LEV - 1) * 4 * per_level
    piece = slices.shape[1]

    def start_all(copies):
        for copy in copies:
            copy.start()

    def at(x_step=0, y_step=0, z_step=0, to_core=None):
        there = core if to_core is None else to_core
        return {
            "sec": (lax.rem(z + z_step, 4) * 4 + lax.rem(x + x_step, 4)) * 2 + there,
            "col": lax.rem(me + y_step, 4),
        }

    partners = [dict(x_step=i) for i in (1, 2, 3)] + [dict(z_step=i) for i in (1, 2, 3)]
    partners += [dict(y_step=j) for j in (1, 2, 3)] + [dict(y_step=j, to_core=1 - core) for j in range(4)]

    def level_rows(level):
        return pl.ds(level * per_level, per_level)

    loads = []
    for level in range(LEV):
        rows = level_rows(level)
        parts = [(coupling.at[rows], coup_v.at[rows]), (diag.at[rows], diag_v.at[rows]), (right_sides.at[rows], rhs_v.at[rows])]
        if level:
            lower = level_rows(level - 1)
            parts.append((off.at[lower], off_v.at[lower]))
        loads.append([pltpu.make_async_copy(a, b, in_sem.at[level, i]) for i, (a, b) in enumerate(parts)])
    start_all(loads[0])

    barrier = pltpu.get_barrier_semaphore()
    for partner in partners:
        pl.semaphore_signal(barrier, inc=1, device_id=at(**partner), device_id_type=MESH)


    def count_of(item):
        return 4 if item in SHIFTED else 2

    def ring(item, slot, p, index, target, own_index=None):
        size = per_level * bs // count_of(item)
        ref = got.at[item, slot, pl.ds(p * size, size)]
        return pltpu.make_async_remote_copy(
            src_ref=ref, dst_ref=ref,
            send_sem=send_sem.at[item, index if own_index is None else own_index], recv_sem=recv_sem.at[item, index],
            device_id={"col": target}, device_id_type=MESH,
        )

    def own_sends(item):
        count = count_of(item)
        copies = []
        for p in range(count):
            copies.append(ring(item, me, p, p, right))
            copies.append(ring(item, me, count - 1 - p, 4 + count - 1 - p, left))
        return copies

    def from_left(item, p):
        return ring(item, left, p, p, right)

    def from_right(item, p):
        return ring(item, right, p, 4 + p, right)

    def to_right(item, p):
        return ring(item, left, p, 8 + p, right)

    def to_left(item, p):
        return ring(item, right, p, 8 + p, left, 12 + p)

    def forward_steps(item):
        if count_of(item) == 2:
            return [(0, True, None), (1, False, None)]
        return [
            (0, True, None), (3, False, None),
            (1, True, left != 2), (2, False, right != 0),
            (2, True, left == 0), (1, False, right == 2),
        ]

    def forward(item):
        for p, rightward, allowed in forward_steps(item):
            (from_left if rightward else from_right)(item, p).wait_recv()
            go = (to_right if rightward else to_left)(item, p)
            if allowed is None:
                go.start()
            else:
                pl.when(allowed)(go.start)

    def finish_near(item):
        from_left(item, count_of(item) - 1).wait_recv()
        from_right(item, 0).wait_recv()

    def finish_far(item):
        for p in range(count_of(item)):
            ring(item, across, p, 8 + p, right).wait_recv()

    def finish(item):
        finish_near(item)
        finish_far(item)

    def ring_sends_end(item):
        for copy in own_sends(item):
            copy.wait_send()
        for p, rightward, allowed in forward_steps(item):
            gone = (to_right if rightward else to_left)(item, p)
            if allowed is None:
                gone.wait_send()
            else:
                pl.when(allowed)(gone.wait_send)

    def to_table(level, chunk, sources=range(4)):
        item = level * CHUNKS + chunk
        first = chunk * positions + level * 4 * per_level

        def body(k, carry):
            for source in sources:
                high, low = split(got[item, source, pl.ds(pl.multiple_of(k * bs, bs), bs), :])
                table[first + source * per_level + k, :, :bs] = high
                table[first + source * per_level + k, :, bs:] = low
            return carry

        lax.fori_loop(0, per_level, body, 0)

    def reduced(row, low_row, chunk, limit=None):
        if chunk == 0:
            current = -coup_v[row]
        else:
            current = rhs_v[row, :, (chunk - 1) * bs : chunk * bs]
        if low_row is None:
            return current
        wide = jnp.zeros((bs, 2 * bs), F32)
        narrow = jnp.zeros((bs, bs), F32)
        for begin in range(0, 16, 4):
            pieces = [split(off_v[low_row, j]) for j in range(begin, begin + 4)]
            places = [pattern[low_row, 0, j] for j in range(begin, begin + 4)]
            if limit is None:
                places = [chunk * positions + place for place in places]
            else:
                places = [jnp.where(place < limit, chunk * positions + place, CHUNKS * positions) for place in places]
            picked = jnp.concatenate([table[place] for place in places], axis=0)
            wide += dot(jnp.concatenate([p[0] for p in pieces], axis=1), picked)
            narrow += dot(jnp.concatenate([p[1] for p in pieces], axis=1), picked[:, :bs])
        return current - (wide[:, :bs] + wide[:, bs:] + narrow)

    def compute(level, chunk):
        def body(k, carry):
            row = level * per_level + k
            solved = dot3(diag_v[row], reduced(row, (level - 1) * per_level + k if level else None, chunk))
            if level < LEV - 1:
                got[level * CHUNKS + chunk, me, pl.ds(pl.multiple_of(k * bs, bs), bs), :] = solved
            else:
                top[chunk, pl.ds(pl.multiple_of(k * bs, bs), bs), :] = solved
            return carry

        lax.fori_loop(0, per_level, body, 0)


    def z_copy(owner, k):
        return pltpu.make_async_remote_copy(
            src_ref=z_made.at[owner, k], dst_ref=z_here.at[k], send_sem=far_send.at[0, owner * per_level + k],
            recv_sem=far_recv.at[0, k], device_id=at(y_step=owner + 1), device_id_type=MESH,
        )

    def z_make(begin, end):
        @pl.when(boundary)
        def _():
            def body(step, carry):
                k, owner = begin + step // 4, lax.rem(step, 4)
                place = below + owner * per_level + k
                which, found = jnp.int32(0), jnp.int32(0)
                for j in range(16):
                    same = (pattern[last_low, 0, j] == place).astype(jnp.int32)
                    which, found = which + j * same, found + same
                block = dot3(diag_v[last_row], off_v[last_low, which])
                z_made[owner, k] = jnp.where(found > 0, -block, jnp.zeros_like(block))
                return carry

            lax.fori_loop(0, 4 * (end - begin), body, 0)
            for k in range(begin, end):
                start_all([z_copy(owner, k) for owner in range(3)])
                z_here[k] = z_made[3, k]

    def z_wait():
        @pl.when(jnp.logical_not(boundary))
        def _():
            for k in range(per_level):
                z_copy(0, k).wait_recv()

    def shared(chunk):
        left_side = jnp.concatenate([z_here[k] for k in range(per_level)], axis=1)
        share[...] = dot3(left_side, got[(LEV - 2) * CHUNKS + chunk, me])

        @pl.when(boundary)
        def _():
            share[...] += dot3(diag_v[last_row], reduced(last_row, last_low, chunk, below))

        return share[...].T


    def far(source, target, phase, index, own_index=None, **step):
        return pltpu.make_async_remote_copy(
            src_ref=source, dst_ref=target,
            send_sem=far_send.at[phase, index if own_index is None else own_index], recv_sem=far_recv.at[phase, index],
            device_id=at(**step), device_id_type=MESH,
        )

    def map_of(which):
        return maps[which].reshape(bs, bs)

    rounds = (1, 2, 3)
    other = 1 - core
    map_scatter = [far(map_cut.at[lax.rem(me + j, 4)], map_parts.at[me], 1, j, y_step=j) for j in rounds]
    map_gather = [far(maps.at[core, me], maps.at[core, me], 2, j, y_step=j) for j in rounds]
    map_swap = far(maps.at[core], maps.at[core], 2, 4, to_core=other)
    pair_round = [far(pairs.at[x], pairs.at[x], 3, j, x_step=j) for j in rounds]
    group_round = [far(groups.at[z], groups.at[z], 4, j, z_step=j) for j in rounds]
    base_scatter = [
        [
            far(base_cut.at[h, lax.rem(me + j, 4)], base_parts.at[core, me], 5 + h, j * 2 + core, j, y_step=j, to_core=h)
            for j in range(4)
        ]
        for h in range(2)
    ]
    slice_round = [far(slices.at[x], slices.at[x], 7, j, x_step=j) for j in rounds]
    sum_round = [far(sums.at[z], sums.at[z], 8, j, z_step=j) for j in rounds]
    mine = core * 4 + me
    end_round = [
        far(ends.at[core if s == 0 else other], entered.at[mine], 9, j * 2 + s, y_step=j, to_core=core if s == 0 else other)
        for j in range(4) for s in range(2) if j or s
    ]
    eye = (lax.broadcasted_iota(jnp.int32, (bs, bs), 0) == lax.broadcasted_iota(jnp.int32, (bs, bs), 1)).astype(F32)
    nothing = jnp.zeros((bs, bs), F32)

    def wait_all(copies):
        for copy in copies:
            copy.wait_recv()

    def maps_scatter():
        value = shared(0)
        for q in range(4):
            map_cut[q] = value[q * piece : (q + 1) * piece]
        start_all(map_scatter)
        map_parts[me] = map_cut[me]

    def maps_gather():
        wait_all(map_scatter)
        maps[core, me] = (map_parts[0] + map_parts[1]) + (map_parts[2] + map_parts[3])
        start_all(map_gather)

    def maps_swap():
        wait_all(map_gather)
        map_swap.start()

    def maps_round():
        map_swap.wait_recv()
        pairs[x] = dot3(map_of(0), map_of(1))
        start_all(pair_round)

    def maps_products():
        wait_all(pair_round)
        after = [None, None, pairs[3], eye]
        after[1] = dot3(pairs[2], pairs[3])
        after[0] = dot3(pairs[1], after[1])
        groups[z] = dot3(pairs[0], after[0])
        start_all(group_round)
        inside = [None, None, jnp.where(x == 3, eye, nothing), nothing]
        for i in (1, 0):
            inside[i] = jnp.where(x == i + 1, eye, dot3(pairs[i + 1], inside[i + 1]))
        lead[...] = jnp.where(x == 0, eye, dot3(pairs[0], inside[0]))
        for i in range(4):
            for j, value in enumerate((after[i], inside[i])):
                high, low = split(value)
                span_high[i * bs : (i + 1) * bs, j * bs : (j + 1) * bs] = high
                span_low[i * bs : (i + 1) * bs, j * bs : (j + 1) * bs] = low

    def maps_reach():
        wait_all(group_round)
        inside = [None, None, jnp.where(z == 3, lead[...], nothing), nothing]
        for i in (1, 0):
            inside[i] = jnp.where(z == i + 1, lead[...], dot3(groups[i + 1], inside[i + 1]))
        for i in range(4):
            high, low = split(inside[i])
            reach_high[i * bs : (i + 1) * bs, :] = high
            reach_low[i * bs : (i + 1) * bs, :] = low

    def bases_scatter(chunk):
        h = chunk - 1
        value = shared(chunk)
        for q in range(4):
            base_cut[h, q] = value[q * piece : (q + 1) * piece]
        start_all(base_scatter[h][1:])

        @pl.when(core != h)
        def _():
            base_scatter[h][0].start()

        @pl.when(core == h)
        def _():
            base_parts[core, me] = base_cut[h, me]

    def slices_start():
        for h in range(2):

            @pl.when(core == h)
            def _(h=h):
                for j in range(4):
                    for source in range(2):
                        if j or source != h:
                            far(base_cut.at[h, 0], base_parts.at[source, lax.rem(me + 4 - j, 4)], 5 + h, j * 2 + source, j).wait_recv()

        even = (base_parts[0, 0] + base_parts[0, 1]) + (base_parts[0, 2] + base_parts[0, 3])
        odd = (base_parts[1, 0] + base_parts[1, 1]) + (base_parts[1, 2] + base_parts[1, 3])
        begun[...] = even
        slices[x] = dot3(even, map_of(1)) + odd
        start_all(slice_round)

    def sums_start():
        wait_all(slice_round)
        joined = jnp.concatenate([slices[i] for i in range(4)], axis=1)
        both = dot_ready(joined, span_high[...], span_low[...])
        sums[z] = both[:, :bs]
        start_all(sum_round)
        ends[0] = both[:, bs:]

    def ends_start():
        wait_all(sum_round)
        joined = jnp.concatenate([sums[i] for i in range(4)], axis=1)
        enter = ends[0] + dot_ready(joined, reach_high[...], reach_low[...])
        ends[0] = enter
        ends[1] = begun[...] + dot3(enter, map_of(0))
        entered[mine] = ends[core]
        start_all(end_round)

    def z_sends_end():
        @pl.when(boundary)
        def _():
            for k in range(per_level):
                for owner in range(3):
                    z_copy(owner, k).wait_send()

    def sends_end(copies):
        for copy in copies:
            copy.wait_send()

    def bases_sends_end():
        for h in range(2):
            sends_end(base_scatter[h][1:])

            @pl.when(core != h)
            def _(h=h):
                base_scatter[h][0].wait_send()


    def enter():
        wait_all(end_round)
        for h in range(2):
            value = jnp.concatenate([entered[h * 4 + q] for q in range(4)], axis=0).T
            high, low = split(value)
            enter_high[:, h * bs : (h + 1) * bs] = high
            enter_low[:, h * bs : (h + 1) * bs] = low

    def correct(level):
        if level < LEV - 1:
            parts = [got[level * CHUNKS + chunk, me] for chunk in range(CHUNKS)]
        else:
            parts = [top[chunk] for chunk in range(CHUNKS)]
        change = dot_ready(parts[0], enter_high[...], enter_low[...])
        for h in range(2):
            value = parts[1 + h] + change[:, h * bs : (h + 1) * bs]
            rhs_v[level_rows(level), :, h * bs : (h + 1) * bs] = value.reshape(per_level, bs, bs)
        writes[level].start()

    writes = [pltpu.make_async_copy(rhs_v.at[level_rows(level)], out.at[level_rows(level)], out_sem.at[level]) for level in range(LEV)]

    table[CHUNKS * positions] = jnp.zeros((bs, 2 * bs), BF16)
    for copy in loads[0]:
        copy.wait()
    for group in loads[1:]:
        start_all(group)
    compute(0, 0)
    pl.semaphore_wait(barrier, len(partners))
    start_all(own_sends(0))
    compute(0, 1)
    for group in loads[1:]:
        for copy in group:
            copy.wait()
    z_make(0, 2)
    forward(0)
    start_all(own_sends(1))
    finish(0)
    to_table(0, 0)
    compute(1, 0)
    z_make(2, 4)
    forward(1)
    start_all(own_sends(3))
    compute(0, 2)
    z_make(4, per_level)
    finish(1)
    to_table(0, 1)
    compute(1, 1)
    forward(3)
    start_all(own_sends(2))
    finish(3)
    to_table(1, 0)
    compute(2, 0)
    z_wait()
    maps_scatter()
    forward(2)
    start_all(own_sends(4))
    finish(2)
    to_table(0, 2)
    compute(1, 2)
    maps_gather()
    forward(4)
    ring_sends_end(0)
    ring_sends_end(1)
    z_sends_end()
    start_all(own_sends(5))
    finish(4)
    to_table(1, 1)
    compute(2, 1)
    bases_scatter(1)
    maps_swap()
    forward(5)
    ring_sends_end(3)
    start_all(own_sends(6))
    maps_round()
    maps_products()
    start_all(own_sends(7))
    finish(5)
    to_table(1, 2)
    compute(2, 2)
    bases_scatter(2)
    forward(6)
    forward(7)
    start_all(own_sends(8))
    ring_sends_end(2)
    ring_sends_end(4)
    sends_end(map_scatter + map_gather + [map_swap] + pair_round + group_round)
    maps_reach()
    slices_start()
    finish(6)
    to_table(2, 0)
    sums_start()
    compute(3, 0)
    ends_start()
    forward(8)
    ring_sends_end(5)
    ring_sends_end(6)
    bases_sends_end()
    sends_end(slice_round)
    finish(7)
    to_table(2, 1)
    compute(3, 1)
    enter()
    for level in range(LEV - 1):
        correct(level)
    finish_near(8)
    to_table(2, 2, (me, left, right))
    finish_far(8)
    to_table(2, 2, (across,))
    compute(3, 2)
    correct(LEV - 1)
    ring_sends_end(7)
    ring_sends_end(8)
    sends_end(sum_round + end_round)
    for copy in writes:
        copy.wait()


def section_solve(right_sides, diag_inverse, coupling, off_blocks, pattern):
    rows, bs, width = right_sides.shape
    per_level = rows // LEV
    items = (LEV - 1) * CHUNKS
    any_space = pl.BlockSpec(memory_space=pl.ANY)
    piece = width // 8
    full = pltpu.VMEM((bs, bs), F32)
    four = pltpu.VMEM((4, bs, bs), F32)
    cut = pltpu.VMEM((4, piece, bs), F32)
    cuts = pltpu.VMEM((2, 4, piece, bs), F32)
    return pl.pallas_call(
        section_kernel,
        out_shape=jax.ShapeDtypeStruct((rows, bs, width), F32),
        in_specs=[pl.BlockSpec(memory_space=pltpu.SMEM)] + [any_space] * 4,
        out_specs=any_space,
        scratch_shapes=[
            pltpu.VMEM((rows, bs, width), F32),
            pltpu.VMEM((rows, bs, bs), F32),
            pltpu.VMEM((rows, bs, bs), F32),
            pltpu.VMEM(off_blocks.shape, F32),
            pltpu.VMEM((items, 4, per_level * bs, bs), F32),
            pltpu.VMEM((CHUNKS * (LEV - 1) * 4 * per_level + 1, bs, 2 * bs), BF16),
            pltpu.VMEM((CHUNKS, per_level * bs, bs), F32),
            pltpu.VMEM((4, per_level, bs, bs), F32),
            pltpu.VMEM((per_level, bs, bs), F32),
            full,
            cut, cut, cuts, four, four, full,
            pltpu.VMEM((4 * bs, 2 * bs), BF16),
            pltpu.VMEM((4 * bs, 2 * bs), BF16),
            pltpu.VMEM((4 * bs, bs), BF16),
            pltpu.VMEM((4 * bs, bs), BF16),
            cuts, cuts,
            pltpu.VMEM((piece, bs), F32),
            cut, cut,
            pltpu.VMEM((2, piece, bs), F32),
            pltpu.VMEM((8, piece, bs), F32),
            pltpu.VMEM((bs, width), BF16),
            pltpu.VMEM((bs, width), BF16),
            pltpu.SemaphoreType.DMA((LEV, 4)),
            pltpu.SemaphoreType.DMA((LEV,)),
            pltpu.SemaphoreType.DMA((items, 16)),
            pltpu.SemaphoreType.DMA((items, 12)),
            pltpu.SemaphoreType.DMA((10, 16)),
            pltpu.SemaphoreType.DMA((10, 16)),
        ],
        compiler_params=pltpu.CompilerParams(collective_id=0, has_side_effects=True, vmem_limit_bytes=58 << 20),
        name="section_solve",
    )(pattern.reshape(pattern.shape[0], 1, pattern.shape[1]), right_sides, diag_inverse, coupling, off_blocks)


def hand_on_kernel(solved, out, held, in_sem, out_sem):
    steps = in_sem.shape[0]
    rows = solved.shape[0] // steps
    loads = [pltpu.make_async_copy(solved.at[pl.ds(i * rows, rows)], held.at[pl.ds(i * rows, rows)], in_sem.at[i]) for i in range(steps)]
    stores = [pltpu.make_async_copy(held.at[pl.ds(i * rows, rows)], out.at[pl.ds(i * rows, rows)], out_sem.at[i]) for i in range(steps)]
    for copy in loads:
        copy.start()
    for load, store in zip(loads, stores):
        load.wait()
        store.start()
    for copy in stores:
        copy.wait()


def hand_on(solved):
    any_space = pl.BlockSpec(memory_space=pl.ANY)
    return pl.pallas_call(
        hand_on_kernel,
        out_shape=jax.ShapeDtypeStruct(solved.shape, F32),
        in_specs=[any_space],
        out_specs=any_space,
        scratch_shapes=[pltpu.VMEM(solved.shape, F32), pltpu.SemaphoreType.DMA((5,)), pltpu.SemaphoreType.DMA((5,))],
        compiler_params=pltpu.CompilerParams(vmem_limit_bytes=58 << 20),
        name="hand_on",
    )(solved)


def per_device(right_sides, diag_inverse, coupling, off_blocks, pattern):
    result = section_solve(right_sides[0, 0], diag_inverse[0, 0], coupling[0, 0], off_blocks[0, 0], pattern[0, 0])
    return hand_on(result)[None, None]


def solution(mesh):
    return jax.shard_map(
        per_device,
        mesh=mesh,
        in_specs=(
            P("sec", "col", None, None, None),
            P("sec", "col", None, None, None),
            P("sec", "col", None, None, None),
            P("sec", "col", None, None, None, None),
            P("sec", "col", None, None),
        ),
        out_specs=P("sec", "col", None, None, None),
        check_vma=False,
    )
```

```python
import functools

import jax
import jax.numpy as jnp
from jax import lax
from jax.experimental import pallas as pl
from jax.experimental.pallas import tpu as pltpu
from jax.sharding import PartitionSpec as P

LEV = 4
CHUNKS = 3
SHIFTED = (0, 1, 3)
MESH = pl.DeviceIdType.MESH
F32 = jnp.float32
BF16 = jnp.bfloat16


def split(value):
    high = value.astype(BF16)
    return high, (value - high.astype(F32)).astype(BF16)


def dot(left, right):
    return jnp.dot(left, right, preferred_element_type=F32)


def dot3(left, right):
    left_high, left_low = split(left)
    right_high, right_low = split(right)
    both = dot(left_high, jnp.concatenate([right_high, right_low], axis=1))
    width = right.shape[1]
    return both[:, :width] + both[:, width:] + dot(left_low, right_high)


def dot_ready(left, high, low):
    left_high, left_low = split(left)
    return dot(left_high, high) + dot(left_high, low) + dot(left_low, high)


def section_kernel(
    pattern, right_sides, diag, coupling, off,
    out,
    rhs_v, diag_v, coup_v, off_v, got, table, top,
    z_made, z_here, share, map_cut, map_parts, maps, pairs, groups, lead,
    span_high, span_low, reach_high, reach_low,
    base_cut, base_parts, begun, slices, sums, ends, entered, enter_high, enter_low,
    in_sem, out_sem, send_sem, recv_sem, far_send, far_recv,
):
    me, sec = lax.axis_index("col"), lax.axis_index("sec")
    core = lax.rem(sec, 2)
    x = lax.rem(sec // 2, 4)
    z = sec // 8
    right, left, across = lax.rem(me + 1, 4), lax.rem(me + 3, 4), lax.rem(me + 2, 4)
    boundary = me == 3
    per_level = diag_v.shape[0] // LEV
    bs = diag_v.shape[1]
    items = (LEV - 1) * CHUNKS
    last_row = LEV * per_level - 1
    last_low = (LEV - 1) * per_level - 1
    below = (LEV - 2) * 4 * per_level
    positions = (LEV - 1) * 4 * per_level
    piece = slices.shape[1]

    def start_all(copies):
        for copy in copies:
            copy.start()

    def at(x_step=0, y_step=0, z_step=0, to_core=None):
        there = core if to_core is None else to_core
        return {
            "sec": (lax.rem(z + z_step, 4) * 4 + lax.rem(x + x_step, 4)) * 2 + there,
            "col": lax.rem(me + y_step, 4),
        }

    partners = [dict(x_step=i) for i in (1, 2, 3)] + [dict(z_step=i) for i in (1, 2, 3)]
    partners += [dict(y_step=j) for j in (1, 2, 3)] + [dict(y_step=j, to_core=1 - core) for j in range(4)]

    def level_rows(level):
        return pl.ds(level * per_level, per_level)

    loads = []
    for level in range(LEV):
        rows = level_rows(level)
        parts = [(coupling.at[rows], coup_v.at[rows]), (diag.at[rows], diag_v.at[rows]), (right_sides.at[rows], rhs_v.at[rows])]
        if level:
            lower = level_rows(level - 1)
            parts.append((off.at[lower], off_v.at[lower]))
        loads.append([pltpu.make_async_copy(a, b, in_sem.at[level, i]) for i, (a, b) in enumerate(parts)])
    barrier = pltpu.get_barrier_semaphore()
    for partner in partners:
        pl.semaphore_signal(barrier, inc=1, device_id=at(**partner), device_id_type=MESH)
    start_all(loads[0])


    def count_of(item):
        return 4 if item in SHIFTED else 2

    def ring(item, slot, p, index, target, own_index=None):
        size = per_level * bs // count_of(item)
        ref = got.at[item, slot, pl.ds(p * size, size)]
        return pltpu.make_async_remote_copy(
            src_ref=ref, dst_ref=ref,
            send_sem=send_sem.at[item, index if own_index is None else own_index], recv_sem=recv_sem.at[item, index],
            device_id={"col": target}, device_id_type=MESH,
        )

    def own_sends(item):
        count = count_of(item)
        copies = []
        for p in range(count):
            copies.append(ring(item, me, p, p, right))
            copies.append(ring(item, me, count - 1 - p, 4 + count - 1 - p, left))
        return copies

    def from_left(item, p):
        return ring(item, left, p, p, right)

    def from_right(item, p):
        return ring(item, right, p, 4 + p, right)

    def to_right(item, p):
        return ring(item, left, p, 8 + p, right)

    def to_left(item, p):
        return ring(item, right, p, 8 + p, left, 12 + p)

    def forward_steps(item):
        if count_of(item) == 2:
            return [(0, True, None), (1, False, None)]
        return [
            (0, True, None), (3, False, None),
            (1, True, left != 2), (2, False, right != 0),
            (2, True, left == 0), (1, False, right == 2),
        ]

    def forward(item):
        for p, rightward, allowed in forward_steps(item):
            (from_left if rightward else from_right)(item, p).wait_recv()
            go = (to_right if rightward else to_left)(item, p)
            if allowed is None:
                go.start()
            else:
                pl.when(allowed)(go.start)

    def finish_near(item):
        from_left(item, count_of(item) - 1).wait_recv()
        from_right(item, 0).wait_recv()

    def finish_far(item):
        for p in range(count_of(item)):
            ring(item, across, p, 8 + p, right).wait_recv()

    def finish(item):
        finish_near(item)
        finish_far(item)

    def ring_sends_end(item):
        for copy in own_sends(item):
            copy.wait_send()
        for p, rightward, allowed in forward_steps(item):
            gone = (to_right if rightward else to_left)(item, p)
            if allowed is None:
                gone.wait_send()
            else:
                pl.when(allowed)(gone.wait_send)

    def to_table(level, chunk, sources=range(4)):
        item = level * CHUNKS + chunk
        first = chunk * positions + level * 4 * per_level

        def body(k, carry):
            for source in sources:
                high, low = split(got[item, source, pl.ds(pl.multiple_of(k * bs, bs), bs), :])
                table[first + source * per_level + k, :, :bs] = high
                table[first + source * per_level + k, :, bs:] = low
            return carry

        lax.fori_loop(0, per_level, body, 0)

    def reduced(row, low_row, chunk, limit=None):
        if chunk == 0:
            current = -coup_v[row]
        else:
            current = rhs_v[row, :, (chunk - 1) * bs : chunk * bs]
        if low_row is None:
            return current
        wide = jnp.zeros((bs, 2 * bs), F32)
        narrow = jnp.zeros((bs, bs), F32)
        for begin in range(0, 16, 4):
            pieces = [split(off_v[low_row, j]) for j in range(begin, begin + 4)]
            places = [pattern[low_row, 0, j] for j in range(begin, begin + 4)]
            if limit is None:
                places = [chunk * positions + place for place in places]
            else:
                places = [jnp.where(place < limit, chunk * positions + place, CHUNKS * positions) for place in places]
            picked = jnp.concatenate([table[place] for place in places], axis=0)
            wide += dot(jnp.concatenate([p[0] for p in pieces], axis=1), picked)
            narrow += dot(jnp.concatenate([p[1] for p in pieces], axis=1), picked[:, :bs])
        return current - (wide[:, :bs] + wide[:, bs:] + narrow)

    def compute(level, chunk):
        def body(k, carry):
            row = level * per_level + k
            solved = dot3(diag_v[row], reduced(row, (level - 1) * per_level + k if level else None, chunk))
            if level < LEV - 1:
                got[level * CHUNKS + chunk, me, pl.ds(pl.multiple_of(k * bs, bs), bs), :] = solved
            else:
                top[chunk, pl.ds(pl.multiple_of(k * bs, bs), bs), :] = solved
            return carry

        lax.fori_loop(0, per_level, body, 0)


    def z_copy(owner, k):
        return pltpu.make_async_remote_copy(
            src_ref=z_made.at[owner, k], dst_ref=z_here.at[k], send_sem=far_send.at[0, owner * per_level + k],
            recv_sem=far_recv.at[0, k], device_id=at(y_step=owner + 1), device_id_type=MESH,
        )

    def z_make(begin, end):
        @pl.when(boundary)
        def _():
            def body(step, carry):
                k, owner = begin + step // 4, lax.rem(step, 4)
                place = below + owner * per_level + k
                which, found = jnp.int32(0), jnp.int32(0)
                for j in range(16):
                    same = (pattern[last_low, 0, j] == place).astype(jnp.int32)
                    which, found = which + j * same, found + same
                block = dot3(diag_v[last_row], off_v[last_low, which])
                z_made[owner, k] = jnp.where(found > 0, -block, jnp.zeros_like(block))
                return carry

            lax.fori_loop(0, 4 * (end - begin), body, 0)
            for k in range(begin, end):
                start_all([z_copy(owner, k) for owner in range(3)])
                z_here[k] = z_made[3, k]

    def z_wait():
        @pl.when(jnp.logical_not(boundary))
        def _():
            for k in range(per_level):
                z_copy(0, k).wait_recv()

    def shared(chunk):
        left_side = jnp.concatenate([z_here[k] for k in range(per_level)], axis=1)
        share[...] = dot3(left_side, got[(LEV - 2) * CHUNKS + chunk, me])

        @pl.when(boundary)
        def _():
            share[...] += dot3(diag_v[last_row], reduced(last_row, last_low, chunk, below))

        return share[...].T


    def far(source, target, phase, index, own_index=None, **step):
        return pltpu.make_async_remote_copy(
            src_ref=source, dst_ref=target,
            send_sem=far_send.at[phase, index if own_index is None else own_index], recv_sem=far_recv.at[phase, index],
            device_id=at(**step), device_id_type=MESH,
        )

    def map_of(which):
        return maps[which].reshape(bs, bs)

    rounds = (1, 2, 3)
    other = 1 - core
    map_scatter = [far(map_cut.at[lax.rem(me + j, 4)], map_parts.at[me], 1, j, y_step=j) for j in rounds]
    map_gather = [far(maps.at[core, me], maps.at[core, me], 2, j, y_step=j) for j in rounds]
    map_swap = far(maps.at[core], maps.at[core], 2, 4, to_core=other)
    pair_round = [far(pairs.at[x], pairs.at[x], 3, j, x_step=j) for j in rounds]
    group_round = [far(groups.at[z], groups.at[z], 4, j, z_step=j) for j in rounds]
    base_scatter = [
        [
            far(base_cut.at[h, lax.rem(me + j, 4)], base_parts.at[core, me], 5 + h, j * 2 + core, j, y_step=j, to_core=h)
            for j in range(4)
        ]
        for h in range(2)
    ]
    slice_round = [far(slices.at[x], slices.at[x], 7, j, x_step=j) for j in rounds]
    sum_round = [far(sums.at[z], sums.at[z], 8, j, z_step=j) for j in rounds]
    mine = core * 4 + me
    end_round = [
        far(ends.at[core if s == 0 else other], entered.at[mine], 9, j * 2 + s, y_step=j, to_core=core if s == 0 else other)
        for j in range(4) for s in range(2) if j or s
    ]
    eye = (lax.broadcasted_iota(jnp.int32, (bs, bs), 0) == lax.broadcasted_iota(jnp.int32, (bs, bs), 1)).astype(F32)
    nothing = jnp.zeros((bs, bs), F32)

    def wait_all(copies):
        for copy in copies:
            copy.wait_recv()

    def maps_scatter():
        value = shared(0)
        for q in range(4):
            map_cut[q] = value[q * piece : (q + 1) * piece]
        start_all(map_scatter)
        map_parts[me] = map_cut[me]

    def maps_gather():
        wait_all(map_scatter)
        maps[core, me] = (map_parts[0] + map_parts[1]) + (map_parts[2] + map_parts[3])
        start_all(map_gather)

    def maps_swap():
        wait_all(map_gather)
        map_swap.start()

    def maps_round():
        map_swap.wait_recv()
        pairs[x] = dot3(map_of(0), map_of(1))
        start_all(pair_round)

    def maps_products():
        wait_all(pair_round)
        after = [None, None, pairs[3], eye]
        after[1] = dot3(pairs[2], pairs[3])
        after[0] = dot3(pairs[1], after[1])
        groups[z] = dot3(pairs[0], after[0])
        start_all(group_round)
        inside = [None, None, jnp.where(x == 3, eye, nothing), nothing]
        for i in (1, 0):
            inside[i] = jnp.where(x == i + 1, eye, dot3(pairs[i + 1], inside[i + 1]))
        lead[...] = jnp.where(x == 0, eye, dot3(pairs[0], inside[0]))
        for i in range(4):
            for j, value in enumerate((after[i], inside[i])):
                high, low = split(value)
                span_high[i * bs : (i + 1) * bs, j * bs : (j + 1) * bs] = high
                span_low[i * bs : (i + 1) * bs, j * bs : (j + 1) * bs] = low

    def maps_reach():
        wait_all(group_round)
        inside = [None, None, jnp.where(z == 3, lead[...], nothing), nothing]
        for i in (1, 0):
            inside[i] = jnp.where(z == i + 1, lead[...], dot3(groups[i + 1], inside[i + 1]))
        for i in range(4):
            high, low = split(inside[i])
            reach_high[i * bs : (i + 1) * bs, :] = high
            reach_low[i * bs : (i + 1) * bs, :] = low

    def bases_scatter(chunk):
        h = chunk - 1
        value = shared(chunk)
        for q in range(4):
            base_cut[h, q] = value[q * piece : (q + 1) * piece]
        start_all(base_scatter[h][1:])

        @pl.when(core != h)
        def _():
            base_scatter[h][0].start()

        @pl.when(core == h)
        def _():
            base_parts[core, me] = base_cut[h, me]

    def slices_start():
        for h in range(2):

            @pl.when(core == h)
            def _(h=h):
                for j in range(4):
                    for source in range(2):
                        if j or source != h:
                            far(base_cut.at[h, 0], base_parts.at[source, lax.rem(me + 4 - j, 4)], 5 + h, j * 2 + source, j).wait_recv()

        even = (base_parts[0, 0] + base_parts[0, 1]) + (base_parts[0, 2] + base_parts[0, 3])
        odd = (base_parts[1, 0] + base_parts[1, 1]) + (base_parts[1, 2] + base_parts[1, 3])
        begun[...] = even
        slices[x] = dot3(even, map_of(1)) + odd
        start_all(slice_round)

    def sums_start():
        wait_all(slice_round)
        joined = jnp.concatenate([slices[i] for i in range(4)], axis=1)
        both = dot_ready(joined, span_high[...], span_low[...])
        sums[z] = both[:, :bs]
        start_all(sum_round)
        ends[0] = both[:, bs:]

    def ends_start():
        wait_all(sum_round)
        joined = jnp.concatenate([sums[i] for i in range(4)], axis=1)
        enter = ends[0] + dot_ready(joined, reach_high[...], reach_low[...])
        ends[0] = enter
        ends[1] = begun[...] + dot3(enter, map_of(0))
        entered[mine] = ends[core]
        start_all(end_round)

    def z_sends_end():
        @pl.when(boundary)
        def _():
            for k in range(per_level):
                for owner in range(3):
                    z_copy(owner, k).wait_send()

    def sends_end(copies):
        for copy in copies:
            copy.wait_send()

    def bases_sends_end():
        for h in range(2):
            sends_end(base_scatter[h][1:])

            @pl.when(core != h)
            def _(h=h):
                base_scatter[h][0].wait_send()


    def enter():
        wait_all(end_round)
        for h in range(2):
            value = jnp.concatenate([entered[h * 4 + q] for q in range(4)], axis=0).T
            high, low = split(value)
            enter_high[:, h * bs : (h + 1) * bs] = high
            enter_low[:, h * bs : (h + 1) * bs] = low

    def correct(level):
        if level < LEV - 1:
            parts = [got[level * CHUNKS + chunk, me] for chunk in range(CHUNKS)]
        else:
            parts = [top[chunk] for chunk in range(CHUNKS)]
        change = dot_ready(parts[0], enter_high[...], enter_low[...])
        for h in range(2):
            value = parts[1 + h] + change[:, h * bs : (h + 1) * bs]
            rhs_v[level_rows(level), :, h * bs : (h + 1) * bs] = value.reshape(per_level, bs, bs)
        writes[level].start()

    writes = [pltpu.make_async_copy(rhs_v.at[level_rows(level)], out.at[level_rows(level)], out_sem.at[level]) for level in range(LEV)]

    for copy in loads[0][:2]:
        copy.wait()
    compute(0, 0)
    pl.semaphore_wait(barrier, len(partners))
    start_all(own_sends(0))
    for group in loads[1:]:
        start_all(group)
    loads[0][2].wait()
    compute(0, 1)
    table[CHUNKS * positions] = jnp.zeros((bs, 2 * bs), BF16)
    forward(0)
    start_all(own_sends(1))
    for group in loads[1:]:
        for copy in group:
            copy.wait()
    z_make(0, 2)
    finish(0)
    to_table(0, 0)
    compute(1, 0)
    forward(1)
    start_all(own_sends(3))
    z_make(2, per_level)
    compute(0, 2)
    finish(1)
    to_table(0, 1)
    compute(1, 1)
    forward(3)
    start_all(own_sends(2))
    finish(3)
    to_table(1, 0)
    compute(2, 0)
    z_wait()
    maps_scatter()
    forward(2)
    start_all(own_sends(4))
    finish(2)
    to_table(0, 2)
    compute(1, 2)
    maps_gather()
    forward(4)
    ring_sends_end(0)
    ring_sends_end(1)
    z_sends_end()
    start_all(own_sends(5))
    finish(4)
    to_table(1, 1)
    compute(2, 1)
    bases_scatter(1)
    maps_swap()
    forward(5)
    ring_sends_end(3)
    start_all(own_sends(6))
    maps_round()
    maps_products()
    start_all(own_sends(7))
    finish(5)
    to_table(1, 2)
    compute(2, 2)
    bases_scatter(2)
    forward(6)
    forward(7)
    start_all(own_sends(8))
    ring_sends_end(2)
    ring_sends_end(4)
    sends_end(map_scatter + map_gather + [map_swap] + pair_round + group_round)
    maps_reach()
    slices_start()
    finish(6)
    to_table(2, 0)
    sums_start()
    compute(3, 0)
    ends_start()
    forward(8)
    ring_sends_end(5)
    ring_sends_end(6)
    bases_sends_end()
    sends_end(slice_round)
    finish(7)
    to_table(2, 1)
    compute(3, 1)
    enter()
    for level in range(LEV - 1):
        correct(level)
    finish_near(8)
    to_table(2, 2, (me, left, right))
    finish_far(8)
    to_table(2, 2, (across,))
    compute(3, 2)
    correct(LEV - 1)
    ring_sends_end(7)
    ring_sends_end(8)
    sends_end(sum_round + end_round)
    for copy in writes:
        copy.wait()


def section_solve(right_sides, diag_inverse, coupling, off_blocks, pattern):
    rows, bs, width = right_sides.shape
    per_level = rows // LEV
    items = (LEV - 1) * CHUNKS
    any_space = pl.BlockSpec(memory_space=pl.ANY)
    piece = width // 8
    full = pltpu.VMEM((bs, bs), F32)
    four = pltpu.VMEM((4, bs, bs), F32)
    cut = pltpu.VMEM((4, piece, bs), F32)
    cuts = pltpu.VMEM((2, 4, piece, bs), F32)
    return pl.pallas_call(
        section_kernel,
        out_shape=jax.ShapeDtypeStruct((rows, bs, width), F32),
        in_specs=[pl.BlockSpec(memory_space=pltpu.SMEM)] + [any_space] * 4,
        out_specs=any_space,
        scratch_shapes=[
            pltpu.VMEM((rows, bs, width), F32),
            pltpu.VMEM((rows, bs, bs), F32),
            pltpu.VMEM((rows, bs, bs), F32),
            pltpu.VMEM(off_blocks.shape, F32),
            pltpu.VMEM((items, 4, per_level * bs, bs), F32),
            pltpu.VMEM((CHUNKS * (LEV - 1) * 4 * per_level + 1, bs, 2 * bs), BF16),
            pltpu.VMEM((CHUNKS, per_level * bs, bs), F32),
            pltpu.VMEM((4, per_level, bs, bs), F32),
            pltpu.VMEM((per_level, bs, bs), F32),
            full,
            cut, cut, cuts, four, four, full,
            pltpu.VMEM((4 * bs, 2 * bs), BF16),
            pltpu.VMEM((4 * bs, 2 * bs), BF16),
            pltpu.VMEM((4 * bs, bs), BF16),
            pltpu.VMEM((4 * bs, bs), BF16),
            cuts, cuts,
            pltpu.VMEM((piece, bs), F32),
            cut, cut,
            pltpu.VMEM((2, piece, bs), F32),
            pltpu.VMEM((8, piece, bs), F32),
            pltpu.VMEM((bs, width), BF16),
            pltpu.VMEM((bs, width), BF16),
            pltpu.SemaphoreType.DMA((LEV, 4)),
            pltpu.SemaphoreType.DMA((LEV,)),
            pltpu.SemaphoreType.DMA((items, 16)),
            pltpu.SemaphoreType.DMA((items, 12)),
            pltpu.SemaphoreType.DMA((10, 16)),
            pltpu.SemaphoreType.DMA((10, 16)),
        ],
        compiler_params=pltpu.CompilerParams(collective_id=0, has_side_effects=True, vmem_limit_bytes=58 << 20),
        name="section_solve",
    )(pattern.reshape(pattern.shape[0], 1, pattern.shape[1]), right_sides, diag_inverse, coupling, off_blocks)


def hand_on_kernel(solved, out, held, in_sem, out_sem):
    steps = in_sem.shape[0]
    rows = solved.shape[0] // steps
    loads = [pltpu.make_async_copy(solved.at[pl.ds(i * rows, rows)], held.at[pl.ds(i * rows, rows)], in_sem.at[i]) for i in range(steps)]
    stores = [pltpu.make_async_copy(held.at[pl.ds(i * rows, rows)], out.at[pl.ds(i * rows, rows)], out_sem.at[i]) for i in range(steps)]
    for copy in loads:
        copy.start()
    for load, store in zip(loads, stores):
        load.wait()
        store.start()
    for copy in stores:
        copy.wait()


def hand_on(solved):
    any_space = pl.BlockSpec(memory_space=pl.ANY)
    return pl.pallas_call(
        hand_on_kernel,
        out_shape=jax.ShapeDtypeStruct(solved.shape, F32),
        in_specs=[any_space],
        out_specs=any_space,
        scratch_shapes=[pltpu.VMEM(solved.shape, F32), pltpu.SemaphoreType.DMA((5,)), pltpu.SemaphoreType.DMA((5,))],
        compiler_params=pltpu.CompilerParams(vmem_limit_bytes=58 << 20),
        name="hand_on",
    )(solved)


def per_device(right_sides, diag_inverse, coupling, off_blocks, pattern):
    result = section_solve(right_sides[0, 0], diag_inverse[0, 0], coupling[0, 0], off_blocks[0, 0], pattern[0, 0])
    return hand_on(result)[None, None]


def solution(mesh):
    return jax.shard_map(
        per_device,
        mesh=mesh,
        in_specs=(
            P("sec", "col", None, None, None),
            P("sec", "col", None, None, None),
            P("sec", "col", None, None, None),
            P("sec", "col", None, None, None, None),
            P("sec", "col", None, None),
        ),
        out_specs=P("sec", "col", None, None, None),
        check_vma=False,
    )
```

```python
import functools

import jax
import jax.numpy as jnp
from jax import lax
from jax.experimental import pallas as pl
from jax.experimental.pallas import tpu as pltpu
from jax.sharding import PartitionSpec as P

LEV = 4
CHUNKS = 3
SHIFTED = (0, 1, 2, 3)
MESH = pl.DeviceIdType.MESH
F32 = jnp.float32
BF16 = jnp.bfloat16


def split(value):
    high = value.astype(BF16)
    return high, (value - high.astype(F32)).astype(BF16)


def dot(left, right):
    return jnp.dot(left, right, preferred_element_type=F32)


def dot3(left, right):
    left_high, left_low = split(left)
    right_high, right_low = split(right)
    both = dot(left_high, jnp.concatenate([right_high, right_low], axis=1))
    width = right.shape[1]
    return both[:, :width] + both[:, width:] + dot(left_low, right_high)


def dot_ready(left, high, low):
    left_high, left_low = split(left)
    return dot(left_high, high) + dot(left_high, low) + dot(left_low, high)


def section_kernel(
    pattern, right_sides, diag, coupling, off,
    out,
    rhs_v, diag_v, coup_v, off_v, got, table, top,
    z_made, z_here, share, map_cut, map_parts, maps, pairs, groups, lead,
    span_high, span_low, reach_high, reach_low,
    base_cut, base_parts, begun, slices, sums, ends, entered, enter_high, enter_low,
    in_sem, out_sem, send_sem, recv_sem, far_send, far_recv,
):
    me, sec = lax.axis_index("col"), lax.axis_index("sec")
    core = lax.rem(sec, 2)
    x = lax.rem(sec // 2, 4)
    z = sec // 8
    right, left, across = lax.rem(me + 1, 4), lax.rem(me + 3, 4), lax.rem(me + 2, 4)
    boundary = me == 3
    per_level = diag_v.shape[0] // LEV
    bs = diag_v.shape[1]
    items = (LEV - 1) * CHUNKS
    last_row = LEV * per_level - 1
    last_low = (LEV - 1) * per_level - 1
    below = (LEV - 2) * 4 * per_level
    positions = (LEV - 1) * 4 * per_level
    piece = slices.shape[1]

    def start_all(copies):
        for copy in copies:
            copy.start()

    def at(x_step=0, y_step=0, z_step=0, to_core=None):
        there = core if to_core is None else to_core
        return {
            "sec": (lax.rem(z + z_step, 4) * 4 + lax.rem(x + x_step, 4)) * 2 + there,
            "col": lax.rem(me + y_step, 4),
        }

    partners = [dict(x_step=i) for i in (1, 2, 3)] + [dict(z_step=i) for i in (1, 2, 3)]
    partners += [dict(y_step=j) for j in (1, 2, 3)] + [dict(y_step=j, to_core=1 - core) for j in range(4)]

    def level_rows(level):
        return pl.ds(level * per_level, per_level)

    loads = []
    for level in range(LEV):
        rows = level_rows(level)
        parts = [(coupling.at[rows], coup_v.at[rows]), (diag.at[rows], diag_v.at[rows]), (right_sides.at[rows], rhs_v.at[rows])]
        if level:
            lower = level_rows(level - 1)
            parts.append((off.at[lower], off_v.at[lower]))
        loads.append([pltpu.make_async_copy(a, b, in_sem.at[level, i]) for i, (a, b) in enumerate(parts)])
    barrier = pltpu.get_barrier_semaphore()
    for partner in partners:
        pl.semaphore_signal(barrier, inc=1, device_id=at(**partner), device_id_type=MESH)
    start_all(loads[0])


    def count_of(item):
        return 4 if item in SHIFTED else 2

    def ring(item, slot, p, index, target, own_index=None):
        size = per_level * bs // count_of(item)
        ref = got.at[item, slot, pl.ds(p * size, size)]
        return pltpu.make_async_remote_copy(
            src_ref=ref, dst_ref=ref,
            send_sem=send_sem.at[item, index if own_index is None else own_index], recv_sem=recv_sem.at[item, index],
            device_id={"col": target}, device_id_type=MESH,
        )

    def own_sends(item):
        count = count_of(item)
        copies = []
        for p in range(count):
            copies.append(ring(item, me, p, p, right))
            copies.append(ring(item, me, count - 1 - p, 4 + count - 1 - p, left))
        return copies

    def from_left(item, p):
        return ring(item, left, p, p, right)

    def from_right(item, p):
        return ring(item, right, p, 4 + p, right)

    def to_right(item, p):
        return ring(item, left, p, 8 + p, right)

    def to_left(item, p):
        return ring(item, right, p, 8 + p, left, 12 + p)

    def forward_steps(item):
        if count_of(item) == 2:
            return [(0, True, None), (1, False, None)]
        return [
            (0, True, None), (3, False, None),
            (1, True, left != 2), (2, False, right != 0),
            (2, True, left == 0), (1, False, right == 2),
        ]

    def forward(item):
        for p, rightward, allowed in forward_steps(item):
            (from_left if rightward else from_right)(item, p).wait_recv()
            go = (to_right if rightward else to_left)(item, p)
            if allowed is None:
                go.start()
            else:
                pl.when(allowed)(go.start)

    def finish_near(item):
        from_left(item, count_of(item) - 1).wait_recv()
        from_right(item, 0).wait_recv()

    def finish_far(item):
        for p in range(count_of(item)):
            ring(item, across, p, 8 + p, right).wait_recv()

    def finish(item):
        finish_near(item)
        finish_far(item)

    def ring_sends_end(item):
        for copy in own_sends(item):
            copy.wait_send()
        for p, rightward, allowed in forward_steps(item):
            gone = (to_right if rightward else to_left)(item, p)
            if allowed is None:
                gone.wait_send()
            else:
                pl.when(allowed)(gone.wait_send)

    def to_table(level, chunk, sources=range(4)):
        item = level * CHUNKS + chunk
        first = chunk * positions + level * 4 * per_level

        def body(k, carry):
            for source in sources:
                high, low = split(got[item, source, pl.ds(pl.multiple_of(k * bs, bs), bs), :])
                table[first + source * per_level + k, :, :bs] = high
                table[first + source * per_level + k, :, bs:] = low
            return carry

        lax.fori_loop(0, per_level, body, 0)

    def reduced(row, low_row, chunk, limit=None):
        if chunk == 0:
            current = -coup_v[row]
        else:
            current = rhs_v[row, :, (chunk - 1) * bs : chunk * bs]
        if low_row is None:
            return current
        wide = jnp.zeros((bs, 2 * bs), F32)
        narrow = jnp.zeros((bs, bs), F32)
        for begin in range(0, 16, 4):
            pieces = [split(off_v[low_row, j]) for j in range(begin, begin + 4)]
            places = [pattern[low_row, 0, j] for j in range(begin, begin + 4)]
            if limit is None:
                places = [chunk * positions + place for place in places]
            else:
                places = [jnp.where(place < limit, chunk * positions + place, CHUNKS * positions) for place in places]
            picked = jnp.concatenate([table[place] for place in places], axis=0)
            wide += dot(jnp.concatenate([p[0] for p in pieces], axis=1), picked)
            narrow += dot(jnp.concatenate([p[1] for p in pieces], axis=1), picked[:, :bs])
        return current - (wide[:, :bs] + wide[:, bs:] + narrow)

    def compute(level, chunk):
        def body(k, carry):
            row = level * per_level + k
            solved = dot3(diag_v[row], reduced(row, (level - 1) * per_level + k if level else None, chunk))
            if level < LEV - 1:
                got[level * CHUNKS + chunk, me, pl.ds(pl.multiple_of(k * bs, bs), bs), :] = solved
            else:
                top[chunk, pl.ds(pl.multiple_of(k * bs, bs), bs), :] = solved
            return carry

        lax.fori_loop(0, per_level, body, 0)


    def z_copy(owner, k):
        return pltpu.make_async_remote_copy(
            src_ref=z_made.at[owner, k], dst_ref=z_here.at[k], send_sem=far_send.at[0, owner * per_level + k],
            recv_sem=far_recv.at[0, k], device_id=at(y_step=owner + 1), device_id_type=MESH,
        )

    def z_make(begin, end):
        @pl.when(boundary)
        def _():
            def body(step, carry):
                k, owner = begin + step // 4, lax.rem(step, 4)
                place = below + owner * per_level + k
                which, found = jnp.int32(0), jnp.int32(0)
                for j in range(16):
                    same = (pattern[last_low, 0, j] == place).astype(jnp.int32)
                    which, found = which + j * same, found + same
                block = dot3(diag_v[last_row], off_v[last_low, which])
                z_made[owner, k] = jnp.where(found > 0, -block, jnp.zeros_like(block))
                return carry

            lax.fori_loop(0, 4 * (end - begin), body, 0)
            for k in range(begin, end):
                start_all([z_copy(owner, k) for owner in range(3)])
                z_here[k] = z_made[3, k]

    def z_wait():
        @pl.when(jnp.logical_not(boundary))
        def _():
            for k in range(per_level):
                z_copy(0, k).wait_recv()

    def shared(chunk):
        left_side = jnp.concatenate([z_here[k] for k in range(per_level)], axis=1)
        share[...] = dot3(left_side, got[(LEV - 2) * CHUNKS + chunk, me])

        @pl.when(boundary)
        def _():
            share[...] += dot3(diag_v[last_row], reduced(last_row, last_low, chunk, below))

        return share[...].T


    def far(source, target, phase, index, own_index=None, **step):
        return pltpu.make_async_remote_copy(
            src_ref=source, dst_ref=target,
            send_sem=far_send.at[phase, index if own_index is None else own_index], recv_sem=far_recv.at[phase, index],
            device_id=at(**step), device_id_type=MESH,
        )

    def map_of(which):
        return maps[which].reshape(bs, bs)

    rounds = (1, 2, 3)
    other = 1 - core
    map_scatter = [far(map_cut.at[lax.rem(me + j, 4)], map_parts.at[me], 1, j, y_step=j) for j in rounds]
    map_gather = [far(maps.at[core, me], maps.at[core, me], 2, j, y_step=j) for j in rounds]
    map_swap = far(maps.at[core], maps.at[core], 2, 4, to_core=other)
    pair_round = [far(pairs.at[x], pairs.at[x], 3, j, x_step=j) for j in rounds]
    group_round = [far(groups.at[z], groups.at[z], 4, j, z_step=j) for j in rounds]
    base_scatter = [
        [
            far(base_cut.at[h, lax.rem(me + j, 4)], base_parts.at[core, me], 5 + h, j * 2 + core, j, y_step=j, to_core=h)
            for j in range(4)
        ]
        for h in range(2)
    ]
    slice_round = [far(slices.at[x], slices.at[x], 7, j, x_step=j) for j in rounds]
    sum_round = [far(sums.at[z], sums.at[z], 8, j, z_step=j) for j in rounds]
    mine = core * 4 + me
    end_round = [
        far(ends.at[core if s == 0 else other], entered.at[mine], 9, j * 2 + s, y_step=j, to_core=core if s == 0 else other)
        for j in range(4) for s in range(2) if j or s
    ]
    eye = (lax.broadcasted_iota(jnp.int32, (bs, bs), 0) == lax.broadcasted_iota(jnp.int32, (bs, bs), 1)).astype(F32)
    nothing = jnp.zeros((bs, bs), F32)

    def wait_all(copies):
        for copy in copies:
            copy.wait_recv()

    def maps_scatter():
        value = shared(0)
        for q in range(4):
            map_cut[q] = value[q * piece : (q + 1) * piece]
        start_all(map_scatter)
        map_parts[me] = map_cut[me]

    def maps_gather():
        wait_all(map_scatter)
        maps[core, me] = (map_parts[0] + map_parts[1]) + (map_parts[2] + map_parts[3])
        start_all(map_gather)

    def maps_swap():
        wait_all(map_gather)
        map_swap.start()

    def maps_round():
        map_swap.wait_recv()
        pairs[x] = dot3(map_of(0), map_of(1))
        start_all(pair_round)

    def maps_products():
        wait_all(pair_round)
        after = [None, None, pairs[3], eye]
        after[1] = dot3(pairs[2], pairs[3])
        after[0] = dot3(pairs[1], after[1])
        groups[z] = dot3(pairs[0], after[0])
        start_all(group_round)
        inside = [None, None, jnp.where(x == 3, eye, nothing), nothing]
        for i in (1, 0):
            inside[i] = jnp.where(x == i + 1, eye, dot3(pairs[i + 1], inside[i + 1]))
        lead[...] = jnp.where(x == 0, eye, dot3(pairs[0], inside[0]))
        for i in range(4):
            for j, value in enumerate((after[i], inside[i])):
                high, low = split(value)
                span_high[i * bs : (i + 1) * bs, j * bs : (j + 1) * bs] = high
                span_low[i * bs : (i + 1) * bs, j * bs : (j + 1) * bs] = low

    def maps_reach():
        wait_all(group_round)
        inside = [None, None, jnp.where(z == 3, lead[...], nothing), nothing]
        for i in (1, 0):
            inside[i] = jnp.where(z == i + 1, lead[...], dot3(groups[i + 1], inside[i + 1]))
        for i in range(4):
            high, low = split(inside[i])
            reach_high[i * bs : (i + 1) * bs, :] = high
            reach_low[i * bs : (i + 1) * bs, :] = low

    def bases_scatter(chunk):
        h = chunk - 1
        value = shared(chunk)
        for q in range(4):
            base_cut[h, q] = value[q * piece : (q + 1) * piece]
        start_all(base_scatter[h][1:])

        @pl.when(core != h)
        def _():
            base_scatter[h][0].start()

        @pl.when(core == h)
        def _():
            base_parts[core, me] = base_cut[h, me]

    def slices_start():
        for h in range(2):

            @pl.when(core == h)
            def _(h=h):
                for j in range(4):
                    for source in range(2):
                        if j or source != h:
                            far(base_cut.at[h, 0], base_parts.at[source, lax.rem(me + 4 - j, 4)], 5 + h, j * 2 + source, j).wait_recv()

        even = (base_parts[0, 0] + base_parts[0, 1]) + (base_parts[0, 2] + base_parts[0, 3])
        odd = (base_parts[1, 0] + base_parts[1, 1]) + (base_parts[1, 2] + base_parts[1, 3])
        begun[...] = even
        slices[x] = dot3(even, map_of(1)) + odd
        start_all(slice_round)

    def sums_start():
        wait_all(slice_round)
        joined = jnp.concatenate([slices[i] for i in range(4)], axis=1)
        both = dot_ready(joined, span_high[...], span_low[...])
        sums[z] = both[:, :bs]
        start_all(sum_round)
        ends[0] = both[:, bs:]

    def ends_start():
        wait_all(sum_round)
        joined = jnp.concatenate([sums[i] for i in range(4)], axis=1)
        enter = ends[0] + dot_ready(joined, reach_high[...], reach_low[...])
        ends[0] = enter
        ends[1] = begun[...] + dot3(enter, map_of(0))
        entered[mine] = ends[core]
        start_all(end_round)

    def z_sends_end():
        @pl.when(boundary)
        def _():
            for k in range(per_level):
                for owner in range(3):
                    z_copy(owner, k).wait_send()

    def sends_end(copies):
        for copy in copies:
            copy.wait_send()

    def bases_sends_end():
        for h in range(2):
            sends_end(base_scatter[h][1:])

            @pl.when(core != h)
            def _(h=h):
                base_scatter[h][0].wait_send()


    def enter():
        wait_all(end_round)
        for h in range(2):
            value = jnp.concatenate([entered[h * 4 + q] for q in range(4)], axis=0).T
            high, low = split(value)
            enter_high[:, h * bs : (h + 1) * bs] = high
            enter_low[:, h * bs : (h + 1) * bs] = low

    def correct(level):
        if level < LEV - 1:
            parts = [got[level * CHUNKS + chunk, me] for chunk in range(CHUNKS)]
        else:
            parts = [top[chunk] for chunk in range(CHUNKS)]
        change = dot_ready(parts[0], enter_high[...], enter_low[...])
        for h in range(2):
            value = parts[1 + h] + change[:, h * bs : (h + 1) * bs]
            rhs_v[level_rows(level), :, h * bs : (h + 1) * bs] = value.reshape(per_level, bs, bs)
        writes[level].start()

    writes = [pltpu.make_async_copy(rhs_v.at[level_rows(level)], out.at[level_rows(level)], out_sem.at[level]) for level in range(LEV)]

    for copy in loads[0][:2]:
        copy.wait()
    compute(0, 0)
    pl.semaphore_wait(barrier, len(partners))
    start_all(own_sends(0))
    for group in loads[1:]:
        start_all(group)
    loads[0][2].wait()
    compute(0, 1)
    table[CHUNKS * positions] = jnp.zeros((bs, 2 * bs), BF16)
    forward(0)
    start_all(own_sends(1))
    for group in loads[1:]:
        for copy in group:
            copy.wait()
    z_make(0, 2)
    finish(0)
    to_table(0, 0)
    compute(1, 0)
    forward(1)
    start_all(own_sends(3))
    z_make(2, per_level)
    compute(0, 2)
    finish(1)
    to_table(0, 1)
    compute(1, 1)
    forward(3)
    start_all(own_sends(2))
    finish(3)
    to_table(1, 0)
    compute(2, 0)
    z_wait()
    maps_scatter()
    forward(2)
    start_all(own_sends(4))
    finish(2)
    to_table(0, 2)
    compute(1, 2)
    maps_gather()
    forward(4)
    ring_sends_end(0)
    ring_sends_end(1)
    z_sends_end()
    start_all(own_sends(5))
    finish(4)
    to_table(1, 1)
    compute(2, 1)
    bases_scatter(1)
    maps_swap()
    forward(5)
    ring_sends_end(3)
    start_all(own_sends(6))
    maps_round()
    maps_products()
    start_all(own_sends(7)[:2])
    finish(5)
    to_table(1, 2)
    compute(2, 2)
    bases_scatter(2)
    start_all(own_sends(7)[2:])
    forward(6)
    forward(7)
    start_all(own_sends(8))
    ring_sends_end(2)
    ring_sends_end(4)
    sends_end(map_scatter + map_gather + [map_swap] + pair_round + group_round)
    maps_reach()
    slices_start()
    finish(6)
    to_table(2, 0)
    sums_start()
    compute(3, 0)
    ends_start()
    forward(8)
    ring_sends_end(5)
    ring_sends_end(6)
    bases_sends_end()
    sends_end(slice_round)
    finish(7)
    to_table(2, 1)
    compute(3, 1)
    enter()
    for level in range(LEV - 1):
        correct(level)
    finish_near(8)
    to_table(2, 2, (me, left, right))
    finish_far(8)
    to_table(2, 2, (across,))
    compute(3, 2)
    correct(LEV - 1)
    ring_sends_end(7)
    ring_sends_end(8)
    sends_end(sum_round + end_round)
    for copy in writes:
        copy.wait()


def section_solve(right_sides, diag_inverse, coupling, off_blocks, pattern):
    rows, bs, width = right_sides.shape
    per_level = rows // LEV
    items = (LEV - 1) * CHUNKS
    any_space = pl.BlockSpec(memory_space=pl.ANY)
    piece = width // 8
    full = pltpu.VMEM((bs, bs), F32)
    four = pltpu.VMEM((4, bs, bs), F32)
    cut = pltpu.VMEM((4, piece, bs), F32)
    cuts = pltpu.VMEM((2, 4, piece, bs), F32)
    return pl.pallas_call(
        section_kernel,
        out_shape=jax.ShapeDtypeStruct((rows, bs, width), F32),
        in_specs=[pl.BlockSpec(memory_space=pltpu.SMEM)] + [any_space] * 4,
        out_specs=any_space,
        scratch_shapes=[
            pltpu.VMEM((rows, bs, width), F32),
            pltpu.VMEM((rows, bs, bs), F32),
            pltpu.VMEM((rows, bs, bs), F32),
            pltpu.VMEM(off_blocks.shape, F32),
            pltpu.VMEM((items, 4, per_level * bs, bs), F32),
            pltpu.VMEM((CHUNKS * (LEV - 1) * 4 * per_level + 1, bs, 2 * bs), BF16),
            pltpu.VMEM((CHUNKS, per_level * bs, bs), F32),
            pltpu.VMEM((4, per_level, bs, bs), F32),
            pltpu.VMEM((per_level, bs, bs), F32),
            full,
            cut, cut, cuts, four, four, full,
            pltpu.VMEM((4 * bs, 2 * bs), BF16),
            pltpu.VMEM((4 * bs, 2 * bs), BF16),
            pltpu.VMEM((4 * bs, bs), BF16),
            pltpu.VMEM((4 * bs, bs), BF16),
            cuts, cuts,
            pltpu.VMEM((piece, bs), F32),
            cut, cut,
            pltpu.VMEM((2, piece, bs), F32),
            pltpu.VMEM((8, piece, bs), F32),
            pltpu.VMEM((bs, width), BF16),
            pltpu.VMEM((bs, width), BF16),
            pltpu.SemaphoreType.DMA((LEV, 4)),
            pltpu.SemaphoreType.DMA((LEV,)),
            pltpu.SemaphoreType.DMA((items, 16)),
            pltpu.SemaphoreType.DMA((items, 12)),
            pltpu.SemaphoreType.DMA((10, 16)),
            pltpu.SemaphoreType.DMA((10, 16)),
        ],
        compiler_params=pltpu.CompilerParams(collective_id=0, has_side_effects=True, vmem_limit_bytes=58 << 20),
        name="section_solve",
    )(pattern.reshape(pattern.shape[0], 1, pattern.shape[1]), right_sides, diag_inverse, coupling, off_blocks)


def hand_on_kernel(solved, out, held, in_sem, out_sem):
    steps = in_sem.shape[0]
    rows = solved.shape[0] // steps
    loads = [pltpu.make_async_copy(solved.at[pl.ds(i * rows, rows)], held.at[pl.ds(i * rows, rows)], in_sem.at[i]) for i in range(steps)]
    stores = [pltpu.make_async_copy(held.at[pl.ds(i * rows, rows)], out.at[pl.ds(i * rows, rows)], out_sem.at[i]) for i in range(steps)]
    for copy in loads:
        copy.start()
    for load, store in zip(loads, stores):
        load.wait()
        store.start()
    for copy in stores:
        copy.wait()


def hand_on(solved):
    any_space = pl.BlockSpec(memory_space=pl.ANY)
    return pl.pallas_call(
        hand_on_kernel,
        out_shape=jax.ShapeDtypeStruct(solved.shape, F32),
        in_specs=[any_space],
        out_specs=any_space,
        scratch_shapes=[pltpu.VMEM(solved.shape, F32), pltpu.SemaphoreType.DMA((5,)), pltpu.SemaphoreType.DMA((5,))],
        compiler_params=pltpu.CompilerParams(vmem_limit_bytes=58 << 20),
        name="hand_on",
    )(solved)


def per_device(right_sides, diag_inverse, coupling, off_blocks, pattern):
    result = section_solve(right_sides[0, 0], diag_inverse[0, 0], coupling[0, 0], off_blocks[0, 0], pattern[0, 0])
    return hand_on(result)[None, None]


def solution(mesh):
    return jax.shard_map(
        per_device,
        mesh=mesh,
        in_specs=(
            P("sec", "col", None, None, None),
            P("sec", "col", None, None, None),
            P("sec", "col", None, None, None),
            P("sec", "col", None, None, None, None),
            P("sec", "col", None, None),
        ),
        out_specs=P("sec", "col", None, None, None),
        check_vma=False,
    )
```

```python
import functools

import jax
import jax.numpy as jnp
from jax import lax
from jax.experimental import pallas as pl
from jax.experimental.pallas import tpu as pltpu
from jax.sharding import PartitionSpec as P

LEV = 4
CHUNKS = 3
SHIFTED = (0, 1, 2, 3)
MESH = pl.DeviceIdType.MESH
F32 = jnp.float32
BF16 = jnp.bfloat16


def split(value):
    high = value.astype(BF16)
    return high, (value - high.astype(F32)).astype(BF16)


def dot(left, right):
    return jnp.dot(left, right, preferred_element_type=F32)


def dot3(left, right):
    left_high, left_low = split(left)
    right_high, right_low = split(right)
    both = dot(left_high, jnp.concatenate([right_high, right_low], axis=1))
    width = right.shape[1]
    return both[:, :width] + both[:, width:] + dot(left_low, right_high)


def dot_ready(left, high, low):
    left_high, left_low = split(left)
    return dot(left_high, high) + dot(left_high, low) + dot(left_low, high)


def section_kernel(
    pattern, right_sides, diag, coupling, off,
    out,
    rhs_v, diag_v, coup_v, off_v, got, table, top,
    z_made, z_here, share, map_cut, map_parts, maps, pairs, groups, lead,
    span_high, span_low, reach_high, reach_low,
    base_cut, base_parts, begun, slices, sums, ends, entered, enter_high, enter_low,
    in_sem, out_sem, send_sem, recv_sem, far_send, far_recv,
):
    me, sec = lax.axis_index("col"), lax.axis_index("sec")
    core = lax.rem(sec, 2)
    x = lax.rem(sec // 2, 4)
    z = sec // 8
    right, left, across = lax.rem(me + 1, 4), lax.rem(me + 3, 4), lax.rem(me + 2, 4)
    boundary = me == 3
    per_level = diag_v.shape[0] // LEV
    bs = diag_v.shape[1]
    items = (LEV - 1) * CHUNKS
    last_row = LEV * per_level - 1
    last_low = (LEV - 1) * per_level - 1
    below = (LEV - 2) * 4 * per_level
    positions = (LEV - 1) * 4 * per_level
    piece = slices.shape[1]

    def start_all(copies):
        for copy in copies:
            copy.start()

    def at(x_step=0, y_step=0, z_step=0, to_core=None):
        there = core if to_core is None else to_core
        return {
            "sec": (lax.rem(z + z_step, 4) * 4 + lax.rem(x + x_step, 4)) * 2 + there,
            "col": lax.rem(me + y_step, 4),
        }

    partners = [dict(x_step=i) for i in (1, 2, 3)] + [dict(z_step=i) for i in (1, 2, 3)]
    partners += [dict(y_step=j) for j in (1, 2, 3)] + [dict(y_step=j, to_core=1 - core) for j in range(4)]

    def level_rows(level):
        return pl.ds(level * per_level, per_level)

    loads = []
    for level in range(LEV):
        rows = level_rows(level)
        parts = [(coupling.at[rows], coup_v.at[rows]), (diag.at[rows], diag_v.at[rows]), (right_sides.at[rows], rhs_v.at[rows])]
        if level:
            lower = level_rows(level - 1)
            parts.append((off.at[lower], off_v.at[lower]))
        loads.append([pltpu.make_async_copy(a, b, in_sem.at[level, i]) for i, (a, b) in enumerate(parts)])
    barrier = pltpu.get_barrier_semaphore()
    for partner in partners:
        pl.semaphore_signal(barrier, inc=1, device_id=at(**partner), device_id_type=MESH)
    start_all(loads[0])


    def count_of(item):
        return 4 if item in SHIFTED else 2

    def ring(item, slot, p, index, target, own_index=None):
        size = per_level * bs // count_of(item)
        ref = got.at[item, slot, pl.ds(p * size, size)]
        return pltpu.make_async_remote_copy(
            src_ref=ref, dst_ref=ref,
            send_sem=send_sem.at[item, index if own_index is None else own_index], recv_sem=recv_sem.at[item, index],
            device_id={"col": target}, device_id_type=MESH,
        )

    def own_sends(item):
        count = count_of(item)
        copies = []
        for p in range(count):
            copies.append(ring(item, me, p, p, right))
            copies.append(ring(item, me, count - 1 - p, 4 + count - 1 - p, left))
        return copies

    def from_left(item, p):
        return ring(item, left, p, p, right)

    def from_right(item, p):
        return ring(item, right, p, 4 + p, right)

    def to_right(item, p):
        return ring(item, left, p, 8 + p, right)

    def to_left(item, p):
        return ring(item, right, p, 8 + p, left, 12 + p)

    def forward_steps(item):
        if count_of(item) == 2:
            return [(0, True, None), (1, False, None)]
        return [
            (0, True, None), (3, False, None),
            (1, True, left != 2), (2, False, right != 0),
            (2, True, left == 0), (1, False, right == 2),
        ]

    def forward(item):
        for p, rightward, allowed in forward_steps(item):
            (from_left if rightward else from_right)(item, p).wait_recv()
            go = (to_right if rightward else to_left)(item, p)
            if allowed is None:
                go.start()
            else:
                pl.when(allowed)(go.start)

    def finish_near(item):
        from_left(item, count_of(item) - 1).wait_recv()
        from_right(item, 0).wait_recv()

    def finish_far(item):
        for p in range(count_of(item)):
            ring(item, across, p, 8 + p, right).wait_recv()

    def finish(item):
        finish_near(item)
        finish_far(item)

    def ring_sends_end(item):
        for copy in own_sends(item):
            copy.wait_send()
        for p, rightward, allowed in forward_steps(item):
            gone = (to_right if rightward else to_left)(item, p)
            if allowed is None:
                gone.wait_send()
            else:
                pl.when(allowed)(gone.wait_send)

    def to_table(level, chunk, sources=range(4)):
        item = level * CHUNKS + chunk
        first = chunk * positions + level * 4 * per_level

        def body(k, carry):
            for source in sources:
                high, low = split(got[item, source, pl.ds(pl.multiple_of(k * bs, bs), bs), :])
                table[first + source * per_level + k, :, :bs] = high
                table[first + source * per_level + k, :, bs:] = low
            return carry

        lax.fori_loop(0, per_level, body, 0)

    def reduced(row, low_row, chunk, limit=None):
        if chunk == 0:
            current = -coup_v[row]
        else:
            current = rhs_v[row, :, (chunk - 1) * bs : chunk * bs]
        if low_row is None:
            return current
        wide = jnp.zeros((bs, 2 * bs), F32)
        narrow = jnp.zeros((bs, bs), F32)
        for begin in range(0, 16, 4):
            pieces = [split(off_v[low_row, j]) for j in range(begin, begin + 4)]
            places = [pattern[low_row, 0, j] for j in range(begin, begin + 4)]
            if limit is None:
                places = [chunk * positions + place for place in places]
            else:
                places = [jnp.where(place < limit, chunk * positions + place, CHUNKS * positions) for place in places]
            picked = jnp.concatenate([table[place] for place in places], axis=0)
            wide += dot(jnp.concatenate([p[0] for p in pieces], axis=1), picked)
            narrow += dot(jnp.concatenate([p[1] for p in pieces], axis=1), picked[:, :bs])
        return current - (wide[:, :bs] + wide[:, bs:] + narrow)

    def compute(level, chunk, start=0, stop=per_level):
        def body(k, carry):
            row = level * per_level + k
            solved = dot3(diag_v[row], reduced(row, (level - 1) * per_level + k if level else None, chunk))
            if level < LEV - 1:
                got[level * CHUNKS + chunk, me, pl.ds(pl.multiple_of(k * bs, bs), bs), :] = solved
            else:
                top[chunk, pl.ds(pl.multiple_of(k * bs, bs), bs), :] = solved
            return carry

        lax.fori_loop(start, stop, body, 0)


    def z_copy(owner, k):
        return pltpu.make_async_remote_copy(
            src_ref=z_made.at[owner, k], dst_ref=z_here.at[k], send_sem=far_send.at[0, owner * per_level + k],
            recv_sem=far_recv.at[0, k], device_id=at(y_step=owner + 1), device_id_type=MESH,
        )

    def z_make(begin, end):
        @pl.when(boundary)
        def _():
            def body(step, carry):
                k, owner = begin + step // 4, lax.rem(step, 4)
                place = below + owner * per_level + k
                which, found = jnp.int32(0), jnp.int32(0)
                for j in range(16):
                    same = (pattern[last_low, 0, j] == place).astype(jnp.int32)
                    which, found = which + j * same, found + same
                block = dot3(diag_v[last_row], off_v[last_low, which])
                z_made[owner, k] = jnp.where(found > 0, -block, jnp.zeros_like(block))
                return carry

            lax.fori_loop(0, 4 * (end - begin), body, 0)
            for k in range(begin, end):
                start_all([z_copy(owner, k) for owner in range(3)])
                z_here[k] = z_made[3, k]

    def z_wait():
        @pl.when(jnp.logical_not(boundary))
        def _():
            for k in range(per_level):
                z_copy(0, k).wait_recv()

    def shared(chunk):
        left_side = jnp.concatenate([z_here[k] for k in range(per_level)], axis=1)
        share[...] = dot3(left_side, got[(LEV - 2) * CHUNKS + chunk, me])

        @pl.when(boundary)
        def _():
            share[...] += dot3(diag_v[last_row], reduced(last_row, last_low, chunk, below))

        return share[...].T


    def far(source, target, phase, index, own_index=None, **step):
        return pltpu.make_async_remote_copy(
            src_ref=source, dst_ref=target,
            send_sem=far_send.at[phase, index if own_index is None else own_index], recv_sem=far_recv.at[phase, index],
            device_id=at(**step), device_id_type=MESH,
        )

    def map_of(which):
        return maps[which].reshape(bs, bs)

    rounds = (1, 2, 3)
    other = 1 - core
    map_scatter = [far(map_cut.at[lax.rem(me + j, 4)], map_parts.at[me], 1, j, y_step=j) for j in rounds]
    map_gather = [far(maps.at[core, me], maps.at[core, me], 2, j, y_step=j) for j in rounds]
    map_swap = far(maps.at[core], maps.at[core], 2, 4, to_core=other)
    pair_round = [far(pairs.at[x], pairs.at[x], 3, j, x_step=j) for j in rounds]
    group_round = [far(groups.at[z], groups.at[z], 4, j, z_step=j) for j in rounds]
    base_scatter = [
        [
            far(base_cut.at[h, lax.rem(me + j, 4)], base_parts.at[core, me], 5 + h, j * 2 + core, j, y_step=j, to_core=h)
            for j in range(4)
        ]
        for h in range(2)
    ]
    slice_round = [far(slices.at[x], slices.at[x], 7, j, x_step=j) for j in rounds]
    sum_round = [far(sums.at[z], sums.at[z], 8, j, z_step=j) for j in rounds]
    mine = core * 4 + me
    end_round = [
        far(ends.at[core if s == 0 else other], entered.at[mine], 9, j * 2 + s, y_step=j, to_core=core if s == 0 else other)
        for j in range(4) for s in range(2) if j or s
    ]
    eye = (lax.broadcasted_iota(jnp.int32, (bs, bs), 0) == lax.broadcasted_iota(jnp.int32, (bs, bs), 1)).astype(F32)
    nothing = jnp.zeros((bs, bs), F32)

    def wait_all(copies):
        for copy in copies:
            copy.wait_recv()

    def maps_scatter():
        value = shared(0)
        for q in range(4):
            map_cut[q] = value[q * piece : (q + 1) * piece]
        start_all(map_scatter)
        map_parts[me] = map_cut[me]

    def maps_gather():
        wait_all(map_scatter)
        maps[core, me] = (map_parts[0] + map_parts[1]) + (map_parts[2] + map_parts[3])
        start_all(map_gather)

    def maps_swap():
        wait_all(map_gather)
        map_swap.start()

    def maps_round():
        map_swap.wait_recv()
        pairs[x] = dot3(map_of(0), map_of(1))
        start_all(pair_round)

    def maps_products():
        wait_all(pair_round)
        after = [None, None, pairs[3], eye]
        after[1] = dot3(pairs[2], pairs[3])
        after[0] = dot3(pairs[1], after[1])
        groups[z] = dot3(pairs[0], after[0])
        start_all(group_round)
        inside = [None, None, jnp.where(x == 3, eye, nothing), nothing]
        for i in (1, 0):
            inside[i] = jnp.where(x == i + 1, eye, dot3(pairs[i + 1], inside[i + 1]))
        lead[...] = jnp.where(x == 0, eye, dot3(pairs[0], inside[0]))
        for i in range(4):
            for j, value in enumerate((after[i], inside[i])):
                high, low = split(value)
                span_high[i * bs : (i + 1) * bs, j * bs : (j + 1) * bs] = high
                span_low[i * bs : (i + 1) * bs, j * bs : (j + 1) * bs] = low

    def maps_reach():
        wait_all(group_round)
        inside = [None, None, jnp.where(z == 3, lead[...], nothing), nothing]
        for i in (1, 0):
            inside[i] = jnp.where(z == i + 1, lead[...], dot3(groups[i + 1], inside[i + 1]))
        for i in range(4):
            high, low = split(inside[i])
            reach_high[i * bs : (i + 1) * bs, :] = high
            reach_low[i * bs : (i + 1) * bs, :] = low

    def bases_scatter(chunk):
        h = chunk - 1
        value = shared(chunk)
        for q in range(4):
            base_cut[h, q] = value[q * piece : (q + 1) * piece]
        start_all(base_scatter[h][1:])

        @pl.when(core != h)
        def _():
            base_scatter[h][0].start()

        @pl.when(core == h)
        def _():
            base_parts[core, me] = base_cut[h, me]

    def slices_start():
        for h in range(2):

            @pl.when(core == h)
            def _(h=h):
                for j in range(4):
                    for source in range(2):
                        if j or source != h:
                            far(base_cut.at[h, 0], base_parts.at[source, lax.rem(me + 4 - j, 4)], 5 + h, j * 2 + source, j).wait_recv()

        even = (base_parts[0, 0] + base_parts[0, 1]) + (base_parts[0, 2] + base_parts[0, 3])
        odd = (base_parts[1, 0] + base_parts[1, 1]) + (base_parts[1, 2] + base_parts[1, 3])
        begun[...] = even
        slices[x] = dot3(even, map_of(1)) + odd
        start_all(slice_round)

    def sums_start():
        wait_all(slice_round)
        joined = jnp.concatenate([slices[i] for i in range(4)], axis=1)
        both = dot_ready(joined, span_high[...], span_low[...])
        sums[z] = both[:, :bs]
        start_all(sum_round)
        ends[0] = both[:, bs:]

    def ends_start():
        wait_all(sum_round)
        joined = jnp.concatenate([sums[i] for i in range(4)], axis=1)
        enter = ends[0] + dot_ready(joined, reach_high[...], reach_low[...])
        ends[0] = enter
        ends[1] = begun[...] + dot3(enter, map_of(0))
        entered[mine] = ends[core]
        start_all(end_round)

    def z_sends_end():
        @pl.when(boundary)
        def _():
            for k in range(per_level):
                for owner in range(3):
                    z_copy(owner, k).wait_send()

    def sends_end(copies):
        for copy in copies:
            copy.wait_send()

    def bases_sends_end():
        for h in range(2):
            sends_end(base_scatter[h][1:])

            @pl.when(core != h)
            def _(h=h):
                base_scatter[h][0].wait_send()


    def enter():
        wait_all(end_round)
        for h in range(2):
            value = jnp.concatenate([entered[h * 4 + q] for q in range(4)], axis=0).T
            high, low = split(value)
            enter_high[:, h * bs : (h + 1) * bs] = high
            enter_low[:, h * bs : (h + 1) * bs] = low

    def correct(level):
        parts = [got[level * CHUNKS + chunk, me] for chunk in range(CHUNKS)]
        change = dot_ready(parts[0], enter_high[...], enter_low[...])
        for h in range(2):
            value = parts[1 + h] + change[:, h * bs : (h + 1) * bs]
            rhs_v[level_rows(level), :, h * bs : (h + 1) * bs] = value.reshape(per_level, bs, bs)
        writes[level].start()

    def correct_top(h):
        change = dot_ready(top[0], enter_high[:, h * bs : (h + 1) * bs], enter_low[:, h * bs : (h + 1) * bs])
        rhs_v[level_rows(LEV - 1), :, h * bs : (h + 1) * bs] = (top[1 + h] + change).reshape(per_level, bs, bs)
        writes[LEV - 1 + h].start()

    writes = [
        pltpu.make_async_copy(rhs_v.at[level_rows(level)], out.at[level_rows(level)], out_sem.at[level]) for level in range(LEV - 1)
    ]
    for h in range(2):
        part = (level_rows(LEV - 1), slice(None), pl.ds(h * bs, bs))
        writes.append(pltpu.make_async_copy(rhs_v.at[part], out.at[part], out_sem.at[LEV - 1 + h]))

    for copy in loads[0][:2]:
        copy.wait()
    compute(0, 0)
    pl.semaphore_wait(barrier, len(partners))
    start_all(own_sends(0))
    for group in loads[1:]:
        start_all(group)
    loads[0][2].wait()
    compute(0, 1)
    table[CHUNKS * positions] = jnp.zeros((bs, 2 * bs), BF16)
    forward(0)
    start_all(own_sends(1))
    for group in loads[1:]:
        for copy in group:
            copy.wait()
    z_make(0, 2)
    finish(0)
    to_table(0, 0)
    compute(1, 0)
    forward(1)
    start_all(own_sends(3))
    z_make(2, per_level)
    compute(0, 2)
    finish(1)
    to_table(0, 1)
    compute(1, 1)
    forward(3)
    start_all(own_sends(2))
    finish(3)
    to_table(1, 0)
    compute(2, 0)
    z_wait()
    maps_scatter()
    forward(2)
    start_all(own_sends(4))
    finish(2)
    to_table(0, 2)
    compute(1, 2)
    maps_gather()
    forward(4)
    ring_sends_end(0)
    ring_sends_end(1)
    z_sends_end()
    start_all(own_sends(5))
    finish(4)
    to_table(1, 1)
    compute(2, 1)
    bases_scatter(1)
    maps_swap()
    forward(5)
    ring_sends_end(3)
    start_all(own_sends(6))
    maps_round()
    maps_products()
    start_all(own_sends(7)[:2])
    finish(5)
    to_table(1, 2)
    compute(2, 2)
    bases_scatter(2)
    start_all(own_sends(7)[2:])
    forward(6)
    forward(7)
    start_all(own_sends(8))
    maps_reach()
    slices_start()
    finish(6)
    to_table(2, 0)
    compute(3, 0, 0, 2)
    sums_start()
    compute(3, 0, 2)
    ends_start()
    forward(8)
    ring_sends_end(2)
    ring_sends_end(4)
    sends_end(map_scatter + map_gather + [map_swap] + pair_round + group_round)
    ring_sends_end(5)
    ring_sends_end(6)
    bases_sends_end()
    sends_end(slice_round)
    finish(7)
    to_table(2, 1)
    compute(3, 1)
    enter()
    for level in range(LEV - 1):
        correct(level)
    correct_top(0)
    finish_near(8)
    to_table(2, 2, (me, left, right))
    finish_far(8)
    to_table(2, 2, (across,))
    compute(3, 2)
    correct_top(1)
    ring_sends_end(7)
    ring_sends_end(8)
    sends_end(sum_round + end_round)
    for copy in writes:
        copy.wait()


def section_solve(right_sides, diag_inverse, coupling, off_blocks, pattern):
    rows, bs, width = right_sides.shape
    per_level = rows // LEV
    items = (LEV - 1) * CHUNKS
    any_space = pl.BlockSpec(memory_space=pl.ANY)
    piece = width // 8
    full = pltpu.VMEM((bs, bs), F32)
    four = pltpu.VMEM((4, bs, bs), F32)
    cut = pltpu.VMEM((4, piece, bs), F32)
    cuts = pltpu.VMEM((2, 4, piece, bs), F32)
    return pl.pallas_call(
        section_kernel,
        out_shape=jax.ShapeDtypeStruct((rows, bs, width), F32),
        in_specs=[pl.BlockSpec(memory_space=pltpu.SMEM)] + [any_space] * 4,
        out_specs=any_space,
        scratch_shapes=[
            pltpu.VMEM((rows, bs, width), F32),
            pltpu.VMEM((rows, bs, bs), F32),
            pltpu.VMEM((rows, bs, bs), F32),
            pltpu.VMEM(off_blocks.shape, F32),
            pltpu.VMEM((items, 4, per_level * bs, bs), F32),
            pltpu.VMEM((CHUNKS * (LEV - 1) * 4 * per_level + 1, bs, 2 * bs), BF16),
            pltpu.VMEM((CHUNKS, per_level * bs, bs), F32),
            pltpu.VMEM((4, per_level, bs, bs), F32),
            pltpu.VMEM((per_level, bs, bs), F32),
            full,
            cut, cut, cuts, four, four, full,
            pltpu.VMEM((4 * bs, 2 * bs), BF16),
            pltpu.VMEM((4 * bs, 2 * bs), BF16),
            pltpu.VMEM((4 * bs, bs), BF16),
            pltpu.VMEM((4 * bs, bs), BF16),
            cuts, cuts,
            pltpu.VMEM((piece, bs), F32),
            cut, cut,
            pltpu.VMEM((2, piece, bs), F32),
            pltpu.VMEM((8, piece, bs), F32),
            pltpu.VMEM((bs, width), BF16),
            pltpu.VMEM((bs, width), BF16),
            pltpu.SemaphoreType.DMA((LEV, 4)),
            pltpu.SemaphoreType.DMA((LEV + 1,)),
            pltpu.SemaphoreType.DMA((items, 16)),
            pltpu.SemaphoreType.DMA((items, 12)),
            pltpu.SemaphoreType.DMA((10, 16)),
            pltpu.SemaphoreType.DMA((10, 16)),
        ],
        compiler_params=pltpu.CompilerParams(collective_id=0, has_side_effects=True, vmem_limit_bytes=58 << 20),
        name="section_solve",
    )(pattern.reshape(pattern.shape[0], 1, pattern.shape[1]), right_sides, diag_inverse, coupling, off_blocks)


def hand_on_kernel(solved, out, held, in_sem, out_sem):
    steps = in_sem.shape[0]
    rows = solved.shape[0] // steps
    loads = [pltpu.make_async_copy(solved.at[pl.ds(i * rows, rows)], held.at[pl.ds(i * rows, rows)], in_sem.at[i]) for i in range(steps)]
    stores = [pltpu.make_async_copy(held.at[pl.ds(i * rows, rows)], out.at[pl.ds(i * rows, rows)], out_sem.at[i]) for i in range(steps)]
    for copy in loads:
        copy.start()
    for load, store in zip(loads, stores):
        load.wait()
        store.start()
    for copy in stores:
        copy.wait()


def hand_on(solved):
    any_space = pl.BlockSpec(memory_space=pl.ANY)
    return pl.pallas_call(
        hand_on_kernel,
        out_shape=jax.ShapeDtypeStruct(solved.shape, F32),
        in_specs=[any_space],
        out_specs=any_space,
        scratch_shapes=[pltpu.VMEM(solved.shape, F32), pltpu.SemaphoreType.DMA((5,)), pltpu.SemaphoreType.DMA((5,))],
        compiler_params=pltpu.CompilerParams(vmem_limit_bytes=58 << 20),
        name="hand_on",
    )(solved)


def per_device(right_sides, diag_inverse, coupling, off_blocks, pattern):
    result = section_solve(right_sides[0, 0], diag_inverse[0, 0], coupling[0, 0], off_blocks[0, 0], pattern[0, 0])
    return hand_on(result)[None, None]


def solution(mesh):
    return jax.shard_map(
        per_device,
        mesh=mesh,
        in_specs=(
            P("sec", "col", None, None, None),
            P("sec", "col", None, None, None),
            P("sec", "col", None, None, None),
            P("sec", "col", None, None, None, None),
            P("sec", "col", None, None),
        ),
        out_specs=P("sec", "col", None, None, None),
        check_vma=False,
    )
```
